1024 devices in a mesh: rows: 256 (over y, z, core), grp: 4 (over x).
Axes of the slice: x: 4, y: 8, z: 16, core: 2. Of those that a mesh axis runs over, the one named last changes fastest.
Arguments:
- a_tiles: bfloat16 [4096, 12, 128, 128], P(('rows', 'grp')), may hold values from -0.75 to 0.75
- a_cols: int32 [4096, 12], P(('rows', 'grp')), may hold values from 0 to 4095, as said below
- p_tiles: bfloat16 [4096, 128, 128], P(('rows', 'grp')), may hold values from -0.5 to 0.5
- p_agg: int32 [4096], P(('rows', 'grp')), may hold values from 0 to 1023, as said below
Outputs:
- coarse_band: float32 [1024, 7, 128, 128], P('rows', None, 'grp')
The draws below stay inside these ranges and needn't reach their ends.
Inputs may be any that keep to these rules, and one draw needn't show every extreme that they name: `a_cols`: the 12 block columns of row i are distinct, include i itself, and lie among the 12 block rows starting at (i // 4 - 1) * 4, taken modulo 4096. p_agg[i] = (i // 4 + e) modulo 1024 with e in -1, 0, 1; e = -1 for the first row of each aligned group of 4 rows, e = 1 for the last, e is 0 or -1 in the first half of the group and 0 or 1 in the second, so rows 1 and 2 of each group (counting from 0) each take e from their own coin.
All inputs are finite; a program needn't handle non-finite values.
Results may differ from the reference program's by a relative error of at most 0.0029.
Values may be sent and summed in bfloat16 or wider, within the bound.
No kernel may reach another device: no remote copies, remote signals or barrier semaphores. Data moves between devices by JAX's collectives and lax.ppermute only.
A program may use at most 32 MiB of HBM per device.

```python
import jax
import jax.numpy as jnp
from jax import lax

BS = 128
KT = 12
RB_DEV = 4
NB = 4096
NCB = 1024


def draw_a_cols(key, part):
    key = jax.random.fold_in(key, 11)
    window = 3 * RB_DEV
    scores = jax.random.randint(key, (NB, window), 0, 1 << 20) * window + jnp.arange(window, dtype=jnp.int32)[None, :]
    row_ids = jnp.arange(NB, dtype=jnp.int32)
    diagonal_pos = RB_DEV + row_ids % RB_DEV
    scores = jnp.where(jnp.arange(window, dtype=jnp.int32)[None, :] == diagonal_pos[:, None], -1, scores)
    order = jnp.argsort(scores, axis=1, stable=True)[:, :KT].astype(jnp.int32)
    start = row_ids // RB_DEV * RB_DEV - RB_DEV
    return jnp.mod(start[:, None] + order, NB).astype(jnp.int32)


def draw_p_agg(key, part):
    key = jax.random.fold_in(key, 23)
    row_ids = jnp.arange(NB, dtype=jnp.int32)
    local = row_ids % RB_DEV
    owner = row_ids // RB_DEV
    coin = jax.random.randint(key, (NB,), 0, 2).astype(jnp.int32)
    margin = max(RB_DEV // 4, 2)
    shift_by = jnp.where(local < margin, -coin, jnp.where(local >= RB_DEV - margin, coin, 0))
    shift_by = jnp.where(local == 0, -1, jnp.where(local == RB_DEV - 1, 1, shift_by))
    return jnp.mod(owner + shift_by, NCB).astype(jnp.int32)


def block_levels(rng, dims, shards, least, largest):
    loudness = 1.0
    for dim, shards_of in shards:
        heights = jax.random.uniform(jax.random.fold_in(jax.random.fold_in(rng, 6), dim), (shards_of,), jnp.float32, least / len(shards), largest / len(shards))
        loudness = loudness * jnp.repeat(jnp.exp(heights), dims[dim] // shards_of).reshape((-1,) + (1,) * (len(dims) - 1 - dim))
    return loudness


def normal_values(rng, extent, spread, limit, pieces=(), kind=jnp.bfloat16):
    entries = jax.random.normal(rng, extent, jnp.float32) * spread
    if len(pieces) > 0:
        entries = block_levels(rng, extent, pieces, -0.22, 0.18) * entries
    return jnp.clip(entries, min=-limit, max=limit).astype(kind)


def setup_inputs(seed: int = 0) -> dict:
    key_of = jax.random.split(jax.random.key(seed), 5)
    a_tiles = normal_values(key_of[0], (NB, KT, BS, BS), 0.125, 0.75, ((0, 1024),))
    a_cols = draw_a_cols(jax.random.fold_in(key_of[4], 71), 0)
    p_tiles = normal_values(key_of[2], (NB, BS, BS), BS ** -0.5, 0.5, ((0, 1024),))
    p_agg = draw_p_agg(jax.random.fold_in(key_of[4], 71), 0)
    return {"a_tiles": a_tiles, "a_cols": a_cols, "p_tiles": p_tiles, "p_agg": p_agg}


def reference(a_tiles, a_cols, p_tiles, p_agg):
    band = jnp.zeros((NCB, 7, BS, BS), jnp.float32)

    def one_device(step, band):
        device = jnp.asarray(step).astype(jnp.int32)
        start = (device * RB_DEV).astype(jnp.int32)
        tiles = lax.dynamic_slice_in_dim(a_tiles, start, RB_DEV, 0)
        columns = lax.dynamic_slice_in_dim(a_cols, start, RB_DEV, 0)
        own_tiles = lax.dynamic_slice_in_dim(p_tiles, start, RB_DEV, 0)
        own_agg = lax.dynamic_slice_in_dim(p_agg, start, RB_DEV, 0)
        fetched = p_tiles[columns]
        products = jnp.einsum("rkxy,rkyz->rkxz", tiles.astype(jnp.float32), fetched.astype(jnp.float32)).astype(jnp.bfloat16)
        products = lax.optimization_barrier(products)
        terms = jnp.einsum("ryx,rkyz->rkxz", own_tiles.astype(jnp.float32), products.astype(jnp.float32))
        row_slot = jnp.mod(own_agg - device + 1, NCB).astype(jnp.int32)
        col_slot = jnp.mod(p_agg[columns] - device + 2, NCB).astype(jnp.int32)
        slot = (row_slot[:, None] * 5 + col_slot).reshape(-1)
        onehot = (jnp.arange(15, dtype=jnp.int32)[:, None] == slot[None, :]).astype(jnp.float32)
        sums = jnp.einsum("um,mxz->uxz", onehot, terms.reshape(-1, BS, BS), precision=lax.Precision.HIGHEST).reshape(3, 5, BS, BS)
        for side in range(3):
            coarse = jnp.mod(device - 1 + side, NCB).astype(jnp.int32)
            anchor = (coarse, jnp.int32(2 - side), jnp.int32(0), jnp.int32(0))
            current = lax.dynamic_slice(band, anchor, (1, 5, BS, BS))
            band = lax.dynamic_update_slice(band, current + sums[side][None], anchor)
        return band

    return lax.fori_loop(0, NCB, one_device, band)
```

```python
import functools

import jax
import jax.numpy as jnp
from jax import lax
from jax.experimental import pallas as pl
from jax.experimental.pallas import tpu as pltpu
from jax.sharding import PartitionSpec as P

BS = 128
RB = 4
KT = 12
HALO = RB * BS + 16
SMEM = pl.BlockSpec(memory_space=pltpu.SMEM)
VMEM = pl.BlockSpec(memory_space=pltpu.VMEM)
LIMIT = 32 << 20


def row_bits(count, agg_ref):
    first = agg_ref[0]
    low = (agg_ref[1] - first) & (count - 1)
    high = ((agg_ref[2] - first) & (count - 1)) - 1
    return low, high


def pack_kernel(count, agg_ref, p_ref, out_ref):
    low, high = row_bits(count, agg_ref)
    out_ref[: RB * BS, :] = p_ref[...].reshape(RB * BS, BS)
    half = lax.broadcasted_iota(jnp.int32, (16, BS), 0) < 8
    out_ref[RB * BS :, :] = jnp.where(half, low, high).astype(jnp.float32).astype(jnp.bfloat16)


def halo_bits(ref):
    flags = ref[RB * BS :, :].astype(jnp.float32)
    return (
        jnp.max(flags[:8, :]).astype(jnp.int32),
        jnp.max(flags[8:, :]).astype(jnp.int32),
    )


def terms_kernel(count, cols_ref, agg_ref, a_ref, p_ref, lo_ref, hi_ref, bnd_ref, out_ref, place, acc, left, weights):
    first = agg_ref[0]
    low, high = row_bits(count, agg_ref)
    for r in range(RB):
        for k in range(KT):
            place[r, (cols_ref[r, k] - first * RB) & (RB * count - 1)] = k

    zero = jnp.zeros((BS, BS), jnp.bfloat16)
    turned = [p_ref[r].astype(jnp.float32).T for r in range(RB)]
    keep1 = (low == 0).astype(jnp.float32)
    keep2 = (high == 0).astype(jnp.float32)
    left[0, :BS, :BS] = turned[0].astype(jnp.bfloat16)
    left[0, :BS, BS:] = (turned[1] * keep1).astype(jnp.bfloat16)
    left[0, BS:, :BS] = zero
    left[0, BS:, BS:] = (turned[1] * (1 - keep1)).astype(jnp.bfloat16)
    left[1, :BS, :BS] = (turned[2] * keep2).astype(jnp.bfloat16)
    left[1, :BS, BS:] = zero
    left[1, BS:, :BS] = (turned[2] * (1 - keep2)).astype(jnp.bfloat16)
    left[1, BS:, BS:] = turned[3].astype(jnp.bfloat16)

    acc[...] = jnp.zeros_like(acc)
    bits = (halo_bits(lo_ref), (low, high), halo_bits(hi_ref))

    for pair in range(6):
        n, top = pair // 2, 2 * (pair % 2)
        tiles = []
        for c in (top, top + 1):
            if n == 1:
                tiles.append(p_ref[c])
            else:
                tiles.append((lo_ref if n == 0 else hi_ref)[c * BS : (c + 1) * BS, :])
        w = weights.at[pair % 2]
        w[:BS, :BS] = tiles[0]
        w[:BS, BS:] = zero
        w[BS:, :BS] = zero
        w[BS:, BS:] = tiles[1]
        lhs = jnp.concatenate(
            [
                jnp.concatenate(
                    [a_ref[r, place[r, n * RB + top]], a_ref[r, place[r, n * RB + top + 1]]], axis=1
                )
                for r in range(RB)
            ],
            axis=0,
        )
        prod = jnp.dot(lhs, w[...], preferred_element_type=jnp.float32).astype(jnp.bfloat16)
        up = jnp.dot(left[0], prod[: 2 * BS], preferred_element_type=jnp.float32)
        down = jnp.dot(left[1], prod[2 * BS :], preferred_element_type=jnp.float32)
        b1, b2 = bits[n]
        slots = (n, n + b1) if top == 0 else (n + 1 + b2, n + 2)
        for c in range(2):
            lanes = slice(c * BS, (c + 1) * BS)
            acc[0, slots[c]] += up[:BS, lanes]
            acc[1, slots[c]] += up[BS:, lanes] + down[:BS, lanes]
            acc[2, slots[c]] += down[BS:, lanes]

    side = jnp.where(((first + 1) & 3) == 0, 0, 2)
    for j in range(5):
        bnd_ref[j] = acc[side, j].astype(jnp.bfloat16)
    for s in range(3):
        for j in range(5):
            block = acc[s, j].astype(jnp.bfloat16)
            for q in range(4):
                out_ref[q, s * 5 + j] = block[q * 32 : (q + 1) * 32, :]


def join_kernel(agg_ref, got_ref, sums_ref, out_ref):
    g = (agg_ref[0] + 1) & 3

    @pl.when(g == 0)
    def _():
        for j in range(5):
            for q in range(4):
                out_ref[q, j] = got_ref[j, q * 32 : (q + 1) * 32, :]

    @pl.when(g == 3)
    def _():
        for j in range(5):
            for q in range(4):
                out_ref[q, 10 + j] = got_ref[j, q * 32 : (q + 1) * 32, :]

    for q in range(4):
        out_ref[q, 5:10] = sums_ref[q, 5:10]

    @pl.when(g != 0)
    def _():
        for q in range(4):
            out_ref[q, :5] = sums_ref[q, :5]

    @pl.when(g != 3)
    def _():
        for q in range(4):
            out_ref[q, 10:] = sums_ref[q, 10:]


def band_kernel(in_ref, out_ref):
    def part(g, s, j):
        return in_ref[g, 5 * s + j].astype(jnp.float32)

    for c in range(4):
        for j in range(7):
            terms = []
            if 1 <= j < 6:
                terms.append(part(c, 1, j - 1))
            if j < 5:
                terms.append(part(c - 1, 2, j) if c > 0 else part(0, 0, j))
            if j >= 2:
                terms.append(part(c + 1, 0, j - 2) if c < 3 else part(3, 2, j - 2))
            total = terms[0]
            for term in terms[1:]:
                total = total + term
            out_ref[c, j] = total


def shards(a_tiles, a_cols, p_tiles, p_agg):
    axes = ("rows", "grp")
    count = lax.axis_size(axes)
    params = pltpu.CompilerParams(vmem_limit_bytes=LIMIT)
    packed = pl.pallas_call(
        functools.partial(pack_kernel, count),
        out_shape=jax.ShapeDtypeStruct((HALO, BS), jnp.bfloat16),
        in_specs=[SMEM, VMEM],
        out_specs=VMEM,
        compiler_params=params,
        name="pack",
    )(p_agg, p_tiles)
    ahead = [(i, (i + 1) % count) for i in range(count)]
    low = lax.ppermute(packed, axes, ahead)
    high = lax.ppermute(packed, axes, [(b, a) for a, b in ahead])
    edge, sums = pl.pallas_call(
        functools.partial(terms_kernel, count),
        out_shape=(
            jax.ShapeDtypeStruct((5, BS, BS), jnp.bfloat16),
            jax.ShapeDtypeStruct((4, 15, 32, BS), jnp.bfloat16),
        ),
        in_specs=[SMEM, SMEM, VMEM, VMEM, VMEM, VMEM],
        out_specs=(VMEM, VMEM),
        scratch_shapes=[
            pltpu.SMEM((RB, KT), jnp.int32),
            pltpu.VMEM((3, 5, BS, BS), jnp.float32),
            pltpu.VMEM((2, 2 * BS, 2 * BS), jnp.bfloat16),
            pltpu.VMEM((2, 2 * BS, 2 * BS), jnp.bfloat16),
        ],
        compiler_params=params,
        name="terms",
    )(a_cols, p_agg, a_tiles, p_tiles, low, high)
    cross = []
    for i in range(0, count, 4):
        cross.append((i, (i - 1) % count))
        cross.append((i + 3, (i + 4) % count))
    got = lax.ppermute(edge, axes, cross)
    joined = pl.pallas_call(
        join_kernel,
        out_shape=jax.ShapeDtypeStruct((4, 15, 32, BS), jnp.bfloat16),
        in_specs=[SMEM, VMEM, VMEM],
        out_specs=VMEM,
        compiler_params=params,
        name="join",
    )(p_agg, got, sums)
    parts = lax.all_to_all(joined, "grp", 0, 0, tiled=True)
    return pl.pallas_call(
        band_kernel,
        out_shape=jax.ShapeDtypeStruct((4, 7, 32, BS), jnp.float32),
        in_specs=[VMEM],
        out_specs=VMEM,
        compiler_params=params,
        name="band",
    )(parts)


def solution(mesh):
    in_specs = (
        P(("rows", "grp"), None, None, None),
        P(("rows", "grp"), None),
        P(("rows", "grp"), None, None),
        P(("rows", "grp")),
    )
    out_specs = P("rows", None, "grp", None)
    return jax.shard_map(shards, mesh=mesh, in_specs=in_specs, out_specs=out_specs, check_vma=False)
```

```python
import functools

import jax
import jax.numpy as jnp
from jax import lax
from jax.experimental import pallas as pl
from jax.experimental.pallas import tpu as pltpu
from jax.sharding import PartitionSpec as P

BS = 128
RB = 4
KT = 12
HALO = RB * BS + 16
HBM = pl.BlockSpec(memory_space=pltpu.HBM)
VMEM = pl.BlockSpec(memory_space=pltpu.VMEM)
LIMIT = 32 << 20


def row_bits(count, agg_ref):
    first = agg_ref[0]
    low = (agg_ref[1] - first) & (count - 1)
    high = ((agg_ref[2] - first) & (count - 1)) - 1
    return low, high


def pack_kernel(count, agg_hbm, p_hbm, out_ref, agg_ref, agg_sem, p_sem):
    agg_copy = pltpu.make_async_copy(agg_hbm, agg_ref, agg_sem)
    agg_copy.start()
    copies = [
        pltpu.make_async_copy(p_hbm.at[r], out_ref.at[pl.ds(r * BS, BS)], p_sem.at[r])
        for r in range(RB)
    ]
    for copy in copies:
        copy.start()
    agg_copy.wait()
    low, high = row_bits(count, agg_ref)
    half = lax.broadcasted_iota(jnp.int32, (16, BS), 0) < 8
    out_ref[RB * BS :, :] = jnp.where(half, low, high).astype(jnp.float32).astype(jnp.bfloat16)
    for copy in copies:
        copy.wait()


def halo_bits(ref):
    flags = ref[RB * BS :, :].astype(jnp.float32)
    return (
        jnp.max(flags[:8, :]).astype(jnp.int32),
        jnp.max(flags[8:, :]).astype(jnp.int32),
    )


def fill_weights(w, tiles_ref, top):
    w[:BS, :BS] = tiles_ref[top * BS : (top + 1) * BS, :]
    w[BS:, BS:] = tiles_ref[(top + 1) * BS : (top + 2) * BS, :]


def clear_weights(weights):
    zero = jnp.zeros((BS, BS), jnp.bfloat16)
    for i in range(weights.shape[0]):
        weights[i, :BS, BS:] = zero
        weights[i, BS:, :BS] = zero


def add_pair(n, top, bits, lhs, w, left, acc):
    prod = jnp.dot(lhs, w[...], preferred_element_type=jnp.float32).astype(jnp.bfloat16)
    up = jnp.dot(left[0], prod[: 2 * BS], preferred_element_type=jnp.float32)
    down = jnp.dot(left[1], prod[2 * BS :], preferred_element_type=jnp.float32)
    b1, b2 = bits
    slots = (n, n + b1) if top == 0 else (n + 1 + b2, n + 2)
    for c in range(2):
        lanes = slice(c * BS, (c + 1) * BS)
        acc[0, slots[c]] += up[:BS, lanes]
        acc[1, slots[c]] += up[BS:, lanes] + down[:BS, lanes]
        acc[2, slots[c]] += down[BS:, lanes]


def near_kernel(
    count, cols_hbm, agg_hbm, a_hbm, p_ref, lhs_ref, left, acc, side_ref,
    cols_ref, agg_ref, place, tiles, weights, sems, a_sems,
):
    cols_copy = pltpu.make_async_copy(cols_hbm, cols_ref, sems.at[0])
    agg_copy = pltpu.make_async_copy(agg_hbm, agg_ref, sems.at[1])
    cols_copy.start()
    agg_copy.start()
    copies = [pltpu.make_async_copy(a_hbm.at[r], tiles.at[r], a_sems.at[r]) for r in range(RB)]
    for copy in copies:
        copy.start()
    clear_weights(weights)
    for i in range(2):
        fill_weights(weights.at[i], p_ref, 2 * i)
    acc[...] = jnp.zeros_like(acc)
    turned = [p_ref[r * BS : (r + 1) * BS, :].astype(jnp.float32).T for r in range(RB)]
    agg_copy.wait()
    first = agg_ref[0]
    low, high = row_bits(count, agg_ref)
    zero = jnp.zeros((BS, BS), jnp.bfloat16)
    keep1 = (low == 0).astype(jnp.float32)
    keep2 = (high == 0).astype(jnp.float32)
    left[0, :BS, :BS] = turned[0].astype(jnp.bfloat16)
    left[0, :BS, BS:] = (turned[1] * keep1).astype(jnp.bfloat16)
    left[0, BS:, :BS] = zero
    left[0, BS:, BS:] = (turned[1] * (1 - keep1)).astype(jnp.bfloat16)
    left[1, :BS, :BS] = (turned[2] * keep2).astype(jnp.bfloat16)
    left[1, :BS, BS:] = zero
    left[1, BS:, :BS] = (turned[2] * (1 - keep2)).astype(jnp.bfloat16)
    left[1, BS:, BS:] = turned[3].astype(jnp.bfloat16)
    side_ref[...] = jnp.full((8, BS), (first + 1) & 3, jnp.int32).astype(jnp.float32)

    cols_copy.wait()
    for r in range(RB):
        for k in range(KT):
            place[r, (cols_ref[r, k] - first * RB) & (RB * count - 1)] = k
    for copy in copies:
        copy.wait()
    for top in (0, 2):
        lhs = jnp.concatenate(
            [
                jnp.concatenate([tiles[r, place[r, RB + top + c]] for c in range(2)], axis=1)
                for r in range(RB)
            ],
            axis=0,
        )
        add_pair(1, top, (low, high), lhs, weights.at[top // 2], left, acc)
    base = ((first + 1) & 1) * 2 * RB
    for i in range(4):
        for r in range(RB):
            for c in range(2):
                col = (base if i < 2 else 2 * RB - base) + 2 * (i % 2) + c
                lhs_ref[i, r * BS : (r + 1) * BS, c * BS : (c + 1) * BS] = tiles[r, place[r, col]]


def add_half(h, slots, lhs, w, left, acc):
    prod = jnp.dot(lhs, w[...], preferred_element_type=jnp.float32).astype(jnp.bfloat16)
    sums = jnp.dot(left[h], prod, preferred_element_type=jnp.float32)
    for c in range(2):
        lanes = slice(c * BS, (c + 1) * BS)
        acc[h, slots[c]] += sums[:BS, lanes]
        acc[h + 1, slots[c]] += sums[BS:, lanes]


def far_half(other, lhs_ref, left, near, side_ref, two_ref, one_ref, acc, weights):
    clear_weights(weights)
    for i in range(4):
        fill_weights(weights.at[i], (one_ref, two_ref)[i // 2], 2 * (i % 2))
    acc[...] = near[...]
    side = jnp.max(side_ref[...]).astype(jnp.int32)
    h = 1 - side // 2 if other else side // 2
    offset = 2 * (side & 1)
    bits = (halo_bits(one_ref), halo_bits(two_ref))
    rows = pl.ds(pl.multiple_of(h * 2 * BS, 2 * BS), 2 * BS)
    for i in range(4):
        n = offset if i < 2 else 2 - offset
        b1, b2 = bits[i // 2]
        slots = (n, n + b1) if i % 2 == 0 else (n + 1 + b2, n + 2)
        add_half(h, slots, lhs_ref[i, rows, :], weights.at[i], left, acc)


def edge_kernel(lhs_ref, left, near, side_ref, two_ref, one_ref, edge_ref, acc, weights):
    far_half(False, lhs_ref, left, near, side_ref, two_ref, one_ref, acc, weights)
    first = side_ref[:1, :] < 2
    for j in range(5):
        edge_ref[j] = jnp.where(first, acc[0, j], acc[2, j]).astype(jnp.bfloat16)


def rest_kernel(lhs_ref, left, near, side_ref, two_ref, one_ref, out_ref, acc, weights):
    far_half(True, lhs_ref, left, near, side_ref, two_ref, one_ref, acc, weights)
    for s in range(3):
        for j in range(5):
            block = acc[s, j].astype(jnp.bfloat16)
            for q in range(4):
                out_ref[q, s * 5 + j] = block[q * 32 : (q + 1) * 32, :]


def join_kernel(side_ref, got_ref, sums_ref, out_ref):
    for side, base in ((0, 0), (3, 10)):
        here = side_ref[:1, :] == side
        for j in range(5):
            for q in range(4):
                new = got_ref[j, q * 32 : (q + 1) * 32, :].astype(jnp.float32)
                old = sums_ref[q, base + j].astype(jnp.float32)
                out_ref[q, base + j] = jnp.where(here, new, old).astype(jnp.bfloat16)
    for q in range(4):
        out_ref[q, 5:10] = sums_ref[q, 5:10]


def band_kernel(in_ref, out_ref):
    def part(g, s, j):
        return in_ref[g, 5 * s + j].astype(jnp.float32)

    for c in range(4):
        for j in range(7):
            terms = []
            if 1 <= j < 6:
                terms.append(part(c, 1, j - 1))
            if j < 5:
                terms.append(part(c - 1, 2, j) if c > 0 else part(0, 0, j))
            if j >= 2:
                terms.append(part(c + 1, 0, j - 2) if c < 3 else part(3, 2, j - 2))
            total = terms[0]
            for term in terms[1:]:
                total = total + term
            out_ref[c, j] = total


def shards(a_tiles, a_cols, p_tiles, p_agg):
    axes = ("rows", "grp")
    count = lax.axis_size(axes)
    params = pltpu.CompilerParams(vmem_limit_bytes=LIMIT)
    a_tiles, a_cols, p_tiles, p_agg = (
        pltpu.with_memory_space_constraint(x, pltpu.HBM) for x in (a_tiles, a_cols, p_tiles, p_agg)
    )
    packed = pl.pallas_call(
        functools.partial(pack_kernel, count),
        out_shape=jax.ShapeDtypeStruct((HALO, BS), jnp.bfloat16),
        in_specs=[HBM, HBM],
        out_specs=VMEM,
        scratch_shapes=[
            pltpu.SMEM((RB,), jnp.int32),
            pltpu.SemaphoreType.DMA,
            pltpu.SemaphoreType.DMA((RB,)),
        ],
        compiler_params=params,
        name="pack",
    )(p_agg, p_tiles)
    outer = [(i, (i + 1 if i % 2 else i - 1) % count) for i in range(count)]
    inner = [(i, i ^ 1) for i in range(count)]
    one = lax.ppermute(packed, axes, outer)
    two = lax.ppermute(packed, axes, inner)
    lhs, left, near, side = pl.pallas_call(
        functools.partial(near_kernel, count),
        out_shape=(
            jax.ShapeDtypeStruct((4, RB * BS, 2 * BS), jnp.bfloat16),
            jax.ShapeDtypeStruct((2, 2 * BS, 2 * BS), jnp.bfloat16),
            jax.ShapeDtypeStruct((3, 5, BS, BS), jnp.float32),
            jax.ShapeDtypeStruct((8, BS), jnp.float32),
        ),
        in_specs=[HBM, HBM, HBM, VMEM],
        out_specs=(VMEM, VMEM, VMEM, VMEM),
        scratch_shapes=[
            pltpu.SMEM((RB, KT), jnp.int32),
            pltpu.SMEM((RB,), jnp.int32),
            pltpu.SMEM((RB, KT), jnp.int32),
            pltpu.VMEM((RB, KT, BS, BS), jnp.bfloat16),
            pltpu.VMEM((2, 2 * BS, 2 * BS), jnp.bfloat16),
            pltpu.SemaphoreType.DMA((2,)),
            pltpu.SemaphoreType.DMA((RB,)),
        ],
        compiler_params=params,
        cost_estimate=pl.CostEstimate(flops=2 * 10**8, bytes_accessed=3 * 10**6, transcendentals=0),
        name="near",
    )(a_cols, p_agg, a_tiles, packed)
    far_in = (lhs, left, near, side, two, one)
    edge, most = pl.pallas_call(
        edge_kernel,
        out_shape=(
            jax.ShapeDtypeStruct((5, BS, BS), jnp.bfloat16),
            jax.ShapeDtypeStruct((3, 5, BS, BS), jnp.float32),
        ),
        in_specs=[VMEM] * 6,
        out_specs=(VMEM, VMEM),
        scratch_shapes=[pltpu.VMEM((4, 2 * BS, 2 * BS), jnp.bfloat16)],
        compiler_params=params,
        name="edge",
    )(*far_in)
    sums = pl.pallas_call(
        rest_kernel,
        out_shape=jax.ShapeDtypeStruct((4, 15, 32, BS), jnp.bfloat16),
        in_specs=[VMEM] * 6,
        out_specs=VMEM,
        scratch_shapes=[
            pltpu.VMEM((3, 5, BS, BS), jnp.float32),
            pltpu.VMEM((4, 2 * BS, 2 * BS), jnp.bfloat16),
        ],
        compiler_params=params,
        cost_estimate=pl.CostEstimate(flops=2 * 10**8, bytes_accessed=3 * 10**6, transcendentals=0),
        name="rest",
    )(lhs, left, most, side, two, one)
    cross = []
    for i in range(0, count, 4):
        cross.append((i, (i - 1) % count))
        cross.append((i + 3, (i + 4) % count))
    got = lax.ppermute(edge, axes, cross)
    joined = pl.pallas_call(
        join_kernel,
        out_shape=jax.ShapeDtypeStruct((4, 15, 32, BS), jnp.bfloat16),
        in_specs=[VMEM, VMEM, VMEM],
        out_specs=VMEM,
        compiler_params=params,
        name="join",
    )(side, got, sums)
    parts = lax.all_to_all(joined, "grp", 0, 0, tiled=True)
    return pl.pallas_call(
        band_kernel,
        out_shape=jax.ShapeDtypeStruct((4, 7, 32, BS), jnp.float32),
        in_specs=[VMEM],
        out_specs=VMEM,
        compiler_params=params,
        name="band",
    )(parts)


def solution(mesh):
    in_specs = (
        P(("rows", "grp"), None, None, None),
        P(("rows", "grp"), None),
        P(("rows", "grp"), None, None),
        P(("rows", "grp")),
    )
    out_specs = P("rows", None, "grp", None)
    return jax.shard_map(shards, mesh=mesh, in_specs=in_specs, out_specs=out_specs, check_vma=False)
```

```python
import functools

import jax
import jax.numpy as jnp
from jax import lax
from jax.experimental import pallas as pl
from jax.experimental.pallas import tpu as pltpu
from jax.sharding import PartitionSpec as P

BS = 128
RB = 4
KT = 12
HALO = RB * BS + 16
HBM = pl.BlockSpec(memory_space=pltpu.HBM)
VMEM = pl.BlockSpec(memory_space=pltpu.VMEM)
LIMIT = 32 << 20


def row_bits(count, agg_ref):
    first = agg_ref[0]
    low = (agg_ref[1] - first) & (count - 1)
    high = ((agg_ref[2] - first) & (count - 1)) - 1
    return low, high


def pack_kernel(count, agg_hbm, p_hbm, out_ref, agg_ref, agg_sem, p_sem):
    agg_copy = pltpu.make_async_copy(agg_hbm, agg_ref, agg_sem)
    agg_copy.start()
    copies = [
        pltpu.make_async_copy(p_hbm.at[r], out_ref.at[pl.ds(r * BS, BS)], p_sem.at[r])
        for r in range(RB)
    ]
    for copy in copies:
        copy.start()
    agg_copy.wait()
    low, high = row_bits(count, agg_ref)
    half = lax.broadcasted_iota(jnp.int32, (16, BS), 0) < 8
    out_ref[RB * BS :, :] = jnp.where(half, low, high).astype(jnp.float32).astype(jnp.bfloat16)
    for copy in copies:
        copy.wait()


def halo_bits(ref):
    flags = ref[RB * BS :, :].astype(jnp.float32)
    return (
        jnp.max(flags[:8, :]).astype(jnp.int32),
        jnp.max(flags[8:, :]).astype(jnp.int32),
    )


def fill_weights(w, tiles_ref, top):
    w[:BS, :BS] = tiles_ref[top * BS : (top + 1) * BS, :]
    w[BS:, BS:] = tiles_ref[(top + 1) * BS : (top + 2) * BS, :]


def clear_weights(weights):
    zero = jnp.zeros((BS, BS), jnp.bfloat16)
    for i in range(weights.shape[0]):
        weights[i, :BS, BS:] = zero
        weights[i, BS:, :BS] = zero


def add_pair(n, top, bits, lhs, w, left, acc):
    prod = jnp.dot(lhs, w[...], preferred_element_type=jnp.float32).astype(jnp.bfloat16)
    up = jnp.dot(left[0], prod[: 2 * BS], preferred_element_type=jnp.float32)
    down = jnp.dot(left[1], prod[2 * BS :], preferred_element_type=jnp.float32)
    slots = pair_slots(n, top, bits)
    for c in range(2):
        lanes = slice(c * BS, (c + 1) * BS)
        acc[0, slots[c]] += up[:BS, lanes]
        acc[1, slots[c]] += up[BS:, lanes] + down[:BS, lanes]
        acc[2, slots[c]] += down[BS:, lanes]


def pair_slots(n, top, bits):
    b1, b2 = bits
    return (n, n + b1) if top == 0 else (n + 1 + b2, n + 2)


def near_kernel(
    count, cols_hbm, agg_hbm, a_hbm, p_ref, two_ref, lhs_ref, left, acc, side_ref,
    cols_ref, agg_ref, place, tiles, weights, sems, a_sems,
):
    cols_copy = pltpu.make_async_copy(cols_hbm, cols_ref, sems.at[0])
    agg_copy = pltpu.make_async_copy(agg_hbm, agg_ref, sems.at[1])
    cols_copy.start()
    agg_copy.start()
    copies = [pltpu.make_async_copy(a_hbm.at[r], tiles.at[r], a_sems.at[r]) for r in range(RB)]
    for copy in copies:
        copy.start()
    clear_weights(weights)
    for i in range(4):
        fill_weights(weights.at[i], (p_ref, two_ref)[i // 2], 2 * (i % 2))
    acc[...] = jnp.zeros_like(acc)
    turned = [p_ref[r * BS : (r + 1) * BS, :].astype(jnp.float32).T for r in range(RB)]
    two_bits = halo_bits(two_ref)
    agg_copy.wait()
    first = agg_ref[0]
    low, high = row_bits(count, agg_ref)
    zero = jnp.zeros((BS, BS), jnp.bfloat16)
    keep1 = (low == 0).astype(jnp.float32)
    keep2 = (high == 0).astype(jnp.float32)
    left[0, :BS, :BS] = turned[0].astype(jnp.bfloat16)
    left[0, :BS, BS:] = (turned[1] * keep1).astype(jnp.bfloat16)
    left[0, BS:, :BS] = zero
    left[0, BS:, BS:] = (turned[1] * (1 - keep1)).astype(jnp.bfloat16)
    left[1, :BS, :BS] = (turned[2] * keep2).astype(jnp.bfloat16)
    left[1, :BS, BS:] = zero
    left[1, BS:, :BS] = (turned[2] * (1 - keep2)).astype(jnp.bfloat16)
    left[1, BS:, BS:] = turned[3].astype(jnp.bfloat16)
    side_ref[...] = jnp.full((8, BS), (first + 1) & 3, jnp.int32).astype(jnp.float32)

    cols_copy.wait()
    for r in range(RB):
        for k in range(KT):
            place[r, (cols_ref[r, k] - first * RB) & (RB * count - 1)] = k
    odd = (first + 1) & 1
    inner = (1 - odd) * 2 * RB
    outer = odd * 2 * RB
    for copy in copies:
        copy.wait()
    for i in range(4):
        start = (RB if i < 2 else inner) + 2 * (i % 2)
        lhs = jnp.concatenate(
            [
                jnp.concatenate([tiles[r, place[r, start + c]] for c in range(2)], axis=1)
                for r in range(RB)
            ],
            axis=0,
        )
        n = 1 if i < 2 else 2 * (1 - odd)
        add_pair(n, 2 * (i % 2), (low, high) if i < 2 else two_bits, lhs, weights.at[i], left, acc)
    for i in range(2):
        for r in range(RB):
            for c in range(2):
                tile = tiles[r, place[r, outer + 2 * i + c]]
                lhs_ref[i, r * BS : (r + 1) * BS, c * BS : (c + 1) * BS] = tile


def edge_kernel(lhs_ref, left, near, side_ref, one_ref, edge_ref, acc, weights):
    clear_weights(weights)
    for i in range(2):
        fill_weights(weights.at[i], one_ref, 2 * i)
    side = jnp.max(side_ref[...]).astype(jnp.int32)
    h = side // 2
    acc[...] = near[2 * h]
    bits = halo_bits(one_ref)
    rows = pl.ds(pl.multiple_of(h * 2 * BS, 2 * BS), 2 * BS)
    part = left[h, pl.ds(pl.multiple_of(h * BS, BS), BS), :]
    for i in range(2):
        prod = jnp.dot(lhs_ref[i, rows, :], weights[i], preferred_element_type=jnp.float32)
        sums = jnp.dot(part, prod.astype(jnp.bfloat16), preferred_element_type=jnp.float32)
        slots = pair_slots(2 * (side & 1), 2 * i, bits)
        for c in range(2):
            acc[slots[c]] += sums[:, c * BS : (c + 1) * BS]
    edge_ref[...] = acc[...].astype(jnp.bfloat16)


def rest_kernel(lhs_ref, left, near, side_ref, one_ref, out_ref, acc, weights):
    clear_weights(weights)
    for i in range(2):
        fill_weights(weights.at[i], one_ref, 2 * i)
    acc[...] = near[...]
    side = jnp.max(side_ref[...]).astype(jnp.int32)
    bits = halo_bits(one_ref)
    for i in range(2):
        add_pair(2 * (side & 1), 2 * i, bits, lhs_ref[i], weights.at[i], left, acc)
    for s in range(3):
        for j in range(5):
            block = acc[s, j].astype(jnp.bfloat16)
            for q in range(4):
                out_ref[q, s * 5 + j] = block[q * 32 : (q + 1) * 32, :]


def join_kernel(side_ref, got_ref, sums_ref, out_ref):
    for side, base in ((0, 0), (3, 10)):
        here = side_ref[:1, :] == side
        for j in range(5):
            for q in range(4):
                new = got_ref[j, q * 32 : (q + 1) * 32, :].astype(jnp.float32)
                old = sums_ref[q, base + j].astype(jnp.float32)
                out_ref[q, base + j] = jnp.where(here, new, old).astype(jnp.bfloat16)
    for q in range(4):
        out_ref[q, 5:10] = sums_ref[q, 5:10]


def band_kernel(in_ref, out_hbm, out_ref, sems):
    def part(g, s, j):
        return in_ref[g, 5 * s + j].astype(jnp.float32)

    copies = []
    for c in range(4):
        for j in range(7):
            terms = []
            if 1 <= j < 6:
                terms.append(part(c, 1, j - 1))
            if j < 5:
                terms.append(part(c - 1, 2, j) if c > 0 else part(3, 2, j))
            if j >= 2:
                terms.append(part(c + 1, 0, j - 2) if c < 3 else part(0, 0, j - 2))
            total = terms[0]
            for term in terms[1:]:
                total = total + term
            out_ref[c, j] = total
        copies.append(pltpu.make_async_copy(out_ref.at[c], out_hbm.at[c], sems.at[c]))
        copies[-1].start()
    for copy in copies:
        copy.wait()


def shards(a_tiles, a_cols, p_tiles, p_agg):
    axes = ("rows", "grp")
    count = lax.axis_size(axes)
    params = pltpu.CompilerParams(vmem_limit_bytes=LIMIT)
    a_tiles, a_cols, p_tiles, p_agg = (
        pltpu.with_memory_space_constraint(x, pltpu.HBM) for x in (a_tiles, a_cols, p_tiles, p_agg)
    )
    packed = pl.pallas_call(
        functools.partial(pack_kernel, count),
        out_shape=jax.ShapeDtypeStruct((HALO, BS), jnp.bfloat16),
        in_specs=[HBM, HBM],
        out_specs=VMEM,
        scratch_shapes=[
            pltpu.SMEM((RB,), jnp.int32),
            pltpu.SemaphoreType.DMA,
            pltpu.SemaphoreType.DMA((RB,)),
        ],
        compiler_params=params,
        name="pack",
    )(p_agg, p_tiles)
    two = lax.ppermute(packed, axes, [(i, i ^ 1) for i in range(count)])
    one = lax.ppermute(packed, axes, [(i, (i + 1 if i % 2 else i - 1) % count) for i in range(count)])
    lhs, left, near, side = pl.pallas_call(
        functools.partial(near_kernel, count),
        out_shape=(
            jax.ShapeDtypeStruct((2, RB * BS, 2 * BS), jnp.bfloat16),
            jax.ShapeDtypeStruct((2, 2 * BS, 2 * BS), jnp.bfloat16),
            jax.ShapeDtypeStruct((3, 5, BS, BS), jnp.float32),
            jax.ShapeDtypeStruct((8, BS), jnp.float32),
        ),
        in_specs=[HBM, HBM, HBM, VMEM, VMEM],
        out_specs=(VMEM, VMEM, VMEM, VMEM),
        scratch_shapes=[
            pltpu.SMEM((RB, KT), jnp.int32),
            pltpu.SMEM((RB,), jnp.int32),
            pltpu.SMEM((RB, KT), jnp.int32),
            pltpu.VMEM((RB, KT, BS, BS), jnp.bfloat16),
            pltpu.VMEM((4, 2 * BS, 2 * BS), jnp.bfloat16),
            pltpu.SemaphoreType.DMA((2,)),
            pltpu.SemaphoreType.DMA((RB,)),
        ],
        compiler_params=params,
        cost_estimate=pl.CostEstimate(flops=2 * 10**8, bytes_accessed=4 * 10**6, transcendentals=0),
        name="near",
    )(a_cols, p_agg, a_tiles, packed, two)
    far = (lhs, left, near, side, one)
    edge = pl.pallas_call(
        edge_kernel,
        out_shape=jax.ShapeDtypeStruct((5, BS, BS), jnp.bfloat16),
        in_specs=[VMEM] * 5,
        out_specs=VMEM,
        scratch_shapes=[
            pltpu.VMEM((5, BS, BS), jnp.float32),
            pltpu.VMEM((2, 2 * BS, 2 * BS), jnp.bfloat16),
        ],
        compiler_params=params,
        name="edge",
    )(*far)
    cross = []
    for i in range(0, count, 4):
        cross.append((i, (i - 4) % count))
        cross.append((i + 3, (i + 7) % count))
    got = lax.ppermute(edge, axes, cross)
    sums = pl.pallas_call(
        rest_kernel,
        out_shape=jax.ShapeDtypeStruct((4, 15, 32, BS), jnp.bfloat16),
        in_specs=[VMEM] * 5,
        out_specs=VMEM,
        scratch_shapes=[
            pltpu.VMEM((3, 5, BS, BS), jnp.float32),
            pltpu.VMEM((2, 2 * BS, 2 * BS), jnp.bfloat16),
        ],
        compiler_params=params,
        cost_estimate=pl.CostEstimate(flops=2 * 10**8, bytes_accessed=3 * 10**6, transcendentals=0),
        name="rest",
    )(*far)
    joined = pl.pallas_call(
        join_kernel,
        out_shape=jax.ShapeDtypeStruct((4, 15, 32, BS), jnp.bfloat16),
        in_specs=[VMEM, VMEM, VMEM],
        out_specs=VMEM,
        compiler_params=params,
        name="join",
    )(side, got, sums)
    parts = lax.all_to_all(joined, "grp", 0, 0, tiled=True)
    return pl.pallas_call(
        band_kernel,
        out_shape=jax.ShapeDtypeStruct((4, 7, 32, BS), jnp.float32),
        in_specs=[VMEM],
        out_specs=HBM,
        scratch_shapes=[
            pltpu.VMEM((4, 7, 32, BS), jnp.float32),
            pltpu.SemaphoreType.DMA((4,)),
        ],
        compiler_params=params,
        name="band",
    )(parts)


def solution(mesh):
    in_specs = (
        P(("rows", "grp"), None, None, None),
        P(("rows", "grp"), None),
        P(("rows", "grp"), None, None),
        P(("rows", "grp")),
    )
    out_specs = P("rows", None, "grp", None)
    return jax.shard_map(shards, mesh=mesh, in_specs=in_specs, out_specs=out_specs, check_vma=False)
```

```python
import functools

import jax
import jax.numpy as jnp
from jax import lax
from jax.experimental import pallas as pl
from jax.experimental.pallas import tpu as pltpu
from jax.sharding import PartitionSpec as P

BS = 128
RB = 4
KT = 12
HALO = RB * BS + 16
HBM = pl.BlockSpec(memory_space=pltpu.HBM)
VMEM = pl.BlockSpec(memory_space=pltpu.VMEM)
LIMIT = 32 << 20


def row_bits(count, agg_ref):
    first = agg_ref[0]
    low = (agg_ref[1] - first) & (count - 1)
    high = ((agg_ref[2] - first) & (count - 1)) - 1
    return low, high


def pack_kernel(count, agg_hbm, p_hbm, out_ref, agg_ref, agg_sem, p_sem):
    agg_copy = pltpu.make_async_copy(agg_hbm, agg_ref, agg_sem)
    agg_copy.start()
    copies = [
        pltpu.make_async_copy(p_hbm.at[r], out_ref.at[pl.ds(r * BS, BS)], p_sem.at[r])
        for r in range(RB)
    ]
    for copy in copies:
        copy.start()
    agg_copy.wait()
    low, high = row_bits(count, agg_ref)
    half = lax.broadcasted_iota(jnp.int32, (16, BS), 0) < 8
    out_ref[RB * BS :, :] = jnp.where(half, low, high).astype(jnp.float32).astype(jnp.bfloat16)
    for copy in copies:
        copy.wait()


def halo_bits(ref):
    flags = ref[RB * BS :, :].astype(jnp.float32)
    return (
        jnp.max(flags[:8, :]).astype(jnp.int32),
        jnp.max(flags[8:, :]).astype(jnp.int32),
    )


def fill_weights(w, tiles_ref, top):
    w[:BS, :BS] = tiles_ref[top * BS : (top + 1) * BS, :]
    w[BS:, BS:] = tiles_ref[(top + 1) * BS : (top + 2) * BS, :]


def clear_weights(weights):
    zero = jnp.zeros((BS, BS), jnp.bfloat16)
    for i in range(weights.shape[0]):
        weights[i, :BS, BS:] = zero
        weights[i, BS:, :BS] = zero


def add_pair(n, top, bits, lhs, w, left, acc):
    prod = jnp.dot(lhs, w[...], preferred_element_type=jnp.float32).astype(jnp.bfloat16)
    up = jnp.dot(left[0], prod[: 2 * BS], preferred_element_type=jnp.float32)
    down = jnp.dot(left[1], prod[2 * BS :], preferred_element_type=jnp.float32)
    slots = pair_slots(n, top, bits)
    for c in range(2):
        lanes = slice(c * BS, (c + 1) * BS)
        acc[0, slots[c]] += up[:BS, lanes]
        acc[1, slots[c]] += up[BS:, lanes] + down[:BS, lanes]
        acc[2, slots[c]] += down[BS:, lanes]


def pair_slots(n, top, bits):
    b1, b2 = bits
    return (n, n + b1) if top == 0 else (n + 1 + b2, n + 2)


def near_kernel(
    count, cols_hbm, agg_hbm, a_hbm, p_ref, two_ref, lhs_ref, left, acc, side_ref,
    cols_ref, agg_ref, place, tiles, weights, sems, a_sems,
):
    cols_copy = pltpu.make_async_copy(cols_hbm, cols_ref, sems.at[0])
    agg_copy = pltpu.make_async_copy(agg_hbm, agg_ref, sems.at[1])
    cols_copy.start()
    agg_copy.start()
    copies = [pltpu.make_async_copy(a_hbm.at[r], tiles.at[r], a_sems.at[r]) for r in range(RB)]
    for copy in copies:
        copy.start()
    clear_weights(weights)
    for i in range(4):
        fill_weights(weights.at[i], (p_ref, two_ref)[i // 2], 2 * (i % 2))
    acc[...] = jnp.zeros_like(acc)
    turned = [p_ref[r * BS : (r + 1) * BS, :].astype(jnp.float32).T for r in range(RB)]
    two_bits = halo_bits(two_ref)
    agg_copy.wait()
    first = agg_ref[0]
    low, high = row_bits(count, agg_ref)
    zero = jnp.zeros((BS, BS), jnp.bfloat16)
    keep1 = (low == 0).astype(jnp.float32)
    keep2 = (high == 0).astype(jnp.float32)
    left[0, :BS, :BS] = turned[0].astype(jnp.bfloat16)
    left[0, :BS, BS:] = (turned[1] * keep1).astype(jnp.bfloat16)
    left[0, BS:, :BS] = zero
    left[0, BS:, BS:] = (turned[1] * (1 - keep1)).astype(jnp.bfloat16)
    left[1, :BS, :BS] = (turned[2] * keep2).astype(jnp.bfloat16)
    left[1, :BS, BS:] = zero
    left[1, BS:, :BS] = (turned[2] * (1 - keep2)).astype(jnp.bfloat16)
    left[1, BS:, BS:] = turned[3].astype(jnp.bfloat16)
    side_ref[...] = jnp.full((8, BS), (first + 1) & 7, jnp.int32).astype(jnp.float32)

    cols_copy.wait()
    for r in range(RB):
        for k in range(KT):
            place[r, (cols_ref[r, k] - first * RB) & (RB * count - 1)] = k
    odd = (first + 1) & 1
    inner = (1 - odd) * 2 * RB
    outer = odd * 2 * RB
    for copy in copies:
        copy.wait()
    for i in range(4):
        start = (RB if i < 2 else inner) + 2 * (i % 2)
        lhs = jnp.concatenate(
            [
                jnp.concatenate([tiles[r, place[r, start + c]] for c in range(2)], axis=1)
                for r in range(RB)
            ],
            axis=0,
        )
        n = 1 if i < 2 else 2 * (1 - odd)
        add_pair(n, 2 * (i % 2), (low, high) if i < 2 else two_bits, lhs, weights.at[i], left, acc)
    for i in range(2):
        for r in range(RB):
            for c in range(2):
                tile = tiles[r, place[r, outer + 2 * i + c]]
                lhs_ref[i, r * BS : (r + 1) * BS, c * BS : (c + 1) * BS] = tile


def far_kernel(lhs_ref, left, near, side_ref, one_ref, out_ref, acc, weights):
    clear_weights(weights)
    for i in range(2):
        fill_weights(weights.at[i], one_ref, 2 * i)
    acc[...] = near[...]
    side = jnp.max(side_ref[...]).astype(jnp.int32)
    bits = halo_bits(one_ref)
    for i in range(2):
        add_pair(2 * (side & 1), 2 * i, bits, lhs_ref[i], weights.at[i], left, acc)
    for s in range(3):
        for j in range(5):
            block = acc[s, j].astype(jnp.bfloat16)
            for q in range(4):
                out_ref[q, s * 5 + j] = block[q * 32 : (q + 1) * 32, :]


def split_kernel(side_ref, in_ref, down_ref, up_ref):
    lower = side_ref[:1, :] < 4
    for j in range(5):
        after = in_ref[3, 10 + j].astype(jnp.float32)
        before = in_ref[0, j].astype(jnp.float32)
        down_ref[j] = jnp.where(lower, after, before).astype(jnp.bfloat16)
        up_ref[j] = jnp.where(lower, before, after).astype(jnp.bfloat16)


def band_kernel(in_ref, out_ref):
    def part(g, s, j):
        return in_ref[g, 5 * s + j].astype(jnp.float32)

    for c in range(4):
        for j in range(7):
            terms = []
            if 1 <= j < 6:
                terms.append(part(c, 1, j - 1))
            if j < 5 and c > 0:
                terms.append(part(c - 1, 2, j))
            if j >= 2 and c < 3:
                terms.append(part(c + 1, 0, j - 2))
            total = terms[0] if terms else jnp.zeros((32, BS), jnp.float32)
            for term in terms[1:]:
                total = total + term
            out_ref[c, j] = total


def finish_kernel(side_ref, band_ref, up_ref, down_ref, out_hbm, rows_ref, sems):
    middle = pltpu.make_async_copy(band_ref.at[pl.ds(1, 2)], out_hbm.at[pl.ds(1, 2)], sems.at[0])
    middle.start()
    lower = side_ref[:1, :] < 4
    copies = [middle]
    for i, (c, first) in enumerate(((0, 0), (3, 2))):
        for j in range(7):
            total = band_ref[c, j]
            if first <= j < first + 5:
                down = down_ref[j - first].astype(jnp.float32)
                up = up_ref[j - first].astype(jnp.float32)
                total = total + (jnp.where(lower, up, down) if c == 0 else jnp.where(lower, down, up))
            rows_ref[i, j] = total
        copies.append(pltpu.make_async_copy(rows_ref.at[i], out_hbm.at[c], sems.at[1 + i]))
        copies[-1].start()
    for copy in copies:
        copy.wait()


def shards(a_tiles, a_cols, p_tiles, p_agg):
    axes = ("rows", "grp")
    count = lax.axis_size(axes)
    params = pltpu.CompilerParams(vmem_limit_bytes=LIMIT)
    a_tiles, a_cols, p_tiles, p_agg = (
        pltpu.with_memory_space_constraint(x, pltpu.HBM) for x in (a_tiles, a_cols, p_tiles, p_agg)
    )
    packed = pl.pallas_call(
        functools.partial(pack_kernel, count),
        out_shape=jax.ShapeDtypeStruct((HALO, BS), jnp.bfloat16),
        in_specs=[HBM, HBM],
        out_specs=VMEM,
        scratch_shapes=[
            pltpu.SMEM((RB,), jnp.int32),
            pltpu.SemaphoreType.DMA,
            pltpu.SemaphoreType.DMA((RB,)),
        ],
        compiler_params=params,
        name="pack",
    )(p_agg, p_tiles)
    two = lax.ppermute(packed, axes, [(i, i ^ 1) for i in range(count)])
    one = lax.ppermute(packed, axes, [(i, (i + 1 if i % 2 else i - 1) % count) for i in range(count)])
    lhs, left, near, side = pl.pallas_call(
        functools.partial(near_kernel, count),
        out_shape=(
            jax.ShapeDtypeStruct((2, RB * BS, 2 * BS), jnp.bfloat16),
            jax.ShapeDtypeStruct((2, 2 * BS, 2 * BS), jnp.bfloat16),
            jax.ShapeDtypeStruct((3, 5, BS, BS), jnp.float32),
            jax.ShapeDtypeStruct((8, BS), jnp.float32),
        ),
        in_specs=[HBM, HBM, HBM, VMEM, VMEM],
        out_specs=(VMEM, VMEM, VMEM, VMEM),
        scratch_shapes=[
            pltpu.SMEM((RB, KT), jnp.int32),
            pltpu.SMEM((RB,), jnp.int32),
            pltpu.SMEM((RB, KT), jnp.int32),
            pltpu.VMEM((RB, KT, BS, BS), jnp.bfloat16),
            pltpu.VMEM((4, 2 * BS, 2 * BS), jnp.bfloat16),
            pltpu.SemaphoreType.DMA((2,)),
            pltpu.SemaphoreType.DMA((RB,)),
        ],
        compiler_params=params,
        cost_estimate=pl.CostEstimate(flops=2 * 10**8, bytes_accessed=4 * 10**6, transcendentals=0),
        name="near",
    )(a_cols, p_agg, a_tiles, packed, two)
    sums = pl.pallas_call(
        far_kernel,
        out_shape=jax.ShapeDtypeStruct((4, 15, 32, BS), jnp.bfloat16),
        in_specs=[VMEM] * 5,
        out_specs=VMEM,
        scratch_shapes=[
            pltpu.VMEM((3, 5, BS, BS), jnp.float32),
            pltpu.VMEM((2, 2 * BS, 2 * BS), jnp.bfloat16),
        ],
        compiler_params=params,
        name="far",
    )(lhs, left, near, side, one)
    parts = lax.all_to_all(sums, "grp", 0, 0, tiled=True)
    down, up = pl.pallas_call(
        split_kernel,
        out_shape=(jax.ShapeDtypeStruct((5, 32, BS), jnp.bfloat16),) * 2,
        in_specs=[VMEM, VMEM],
        out_specs=(VMEM, VMEM),
        compiler_params=params,
        name="split",
    )(side, parts)
    got_up = lax.ppermute(up, axes, [(i, (i + 4 if i & 4 else i - 4) % count) for i in range(count)])
    got_down = lax.ppermute(down, axes, [(i, i ^ 4) for i in range(count)])
    band = pl.pallas_call(
        band_kernel,
        out_shape=jax.ShapeDtypeStruct((4, 7, 32, BS), jnp.float32),
        in_specs=[VMEM],
        out_specs=VMEM,
        compiler_params=params,
        cost_estimate=pl.CostEstimate(flops=10**7, bytes_accessed=2 * 10**6, transcendentals=0),
        name="band",
    )(parts)
    return pl.pallas_call(
        finish_kernel,
        out_shape=jax.ShapeDtypeStruct((4, 7, 32, BS), jnp.float32),
        in_specs=[VMEM] * 4,
        out_specs=HBM,
        scratch_shapes=[
            pltpu.VMEM((2, 7, 32, BS), jnp.float32),
            pltpu.SemaphoreType.DMA((3,)),
        ],
        compiler_params=params,
        name="finish",
    )(side, band, got_up, got_down)


def solution(mesh):
    in_specs = (
        P(("rows", "grp"), None, None, None),
        P(("rows", "grp"), None),
        P(("rows", "grp"), None, None),
        P(("rows", "grp")),
    )
    out_specs = P("rows", None, "grp", None)
    return jax.shard_map(shards, mesh=mesh, in_specs=in_specs, out_specs=out_specs, check_vma=False)
```

```python
import functools

import jax
import jax.numpy as jnp
from jax import lax
from jax.experimental import pallas as pl
from jax.experimental.pallas import tpu as pltpu
from jax.sharding import PartitionSpec as P

BS = 128
RB = 4
KT = 12
HALO = RB * BS + 16
HBM = pl.BlockSpec(memory_space=pltpu.HBM)
VMEM = pl.BlockSpec(memory_space=pltpu.VMEM)
LIMIT = 32 << 20


def row_bits(count, agg_ref):
    first = agg_ref[0]
    low = (agg_ref[1] - first) & (count - 1)
    high = ((agg_ref[2] - first) & (count - 1)) - 1
    return low, high


def pack_kernel(count, agg_hbm, p_hbm, out_ref, agg_ref, agg_sem, p_sem):
    agg_copy = pltpu.make_async_copy(agg_hbm, agg_ref, agg_sem)
    agg_copy.start()
    copies = [
        pltpu.make_async_copy(p_hbm.at[r], out_ref.at[pl.ds(r * BS, BS)], p_sem.at[r])
        for r in range(RB)
    ]
    for copy in copies:
        copy.start()
    agg_copy.wait()
    low, high = row_bits(count, agg_ref)
    half = lax.broadcasted_iota(jnp.int32, (16, BS), 0) < 8
    out_ref[RB * BS :, :] = jnp.where(half, low, high).astype(jnp.float32).astype(jnp.bfloat16)
    for copy in copies:
        copy.wait()


def halo_bits(ref):
    flags = ref[RB * BS :, :].astype(jnp.float32)
    return (
        jnp.max(flags[:8, :]).astype(jnp.int32),
        jnp.max(flags[8:, :]).astype(jnp.int32),
    )


def fill_weights(w, tiles_ref, top):
    w[:BS, :BS] = tiles_ref[top * BS : (top + 1) * BS, :]
    w[BS:, BS:] = tiles_ref[(top + 1) * BS : (top + 2) * BS, :]


def clear_weights(weights):
    zero = jnp.zeros((BS, BS), jnp.bfloat16)
    for i in range(weights.shape[0]):
        weights[i, :BS, BS:] = zero
        weights[i, BS:, :BS] = zero


def add_pair(n, top, bits, lhs, w, left, acc):
    prod = jnp.dot(lhs, w[...], preferred_element_type=jnp.float32).astype(jnp.bfloat16)
    up = jnp.dot(left[0], prod[: 2 * BS], preferred_element_type=jnp.float32)
    down = jnp.dot(left[1], prod[2 * BS :], preferred_element_type=jnp.float32)
    slots = pair_slots(n, top, bits)
    for c in range(2):
        lanes = slice(c * BS, (c + 1) * BS)
        acc[0, slots[c]] += up[:BS, lanes]
        acc[1, slots[c]] += up[BS:, lanes] + down[:BS, lanes]
        acc[2, slots[c]] += down[BS:, lanes]


def pair_slots(n, top, bits):
    b1, b2 = bits
    return (n, n + b1) if top == 0 else (n + 1 + b2, n + 2)


def near_kernel(
    count, cols_hbm, agg_hbm, a_hbm, p_ref, one_ref, lhs_ref, left, acc, side_ref,
    cols_ref, agg_ref, place, tiles, weights, sems, a_sems,
):
    cols_copy = pltpu.make_async_copy(cols_hbm, cols_ref, sems.at[0])
    agg_copy = pltpu.make_async_copy(agg_hbm, agg_ref, sems.at[1])
    cols_copy.start()
    agg_copy.start()
    copies = [pltpu.make_async_copy(a_hbm.at[r], tiles.at[r], a_sems.at[r]) for r in range(RB)]
    for copy in copies:
        copy.start()
    clear_weights(weights)
    for i in range(4):
        fill_weights(weights.at[i], (p_ref, one_ref)[i // 2], 2 * (i % 2))
    acc[...] = jnp.zeros_like(acc)
    turned = [p_ref[r * BS : (r + 1) * BS, :].astype(jnp.float32).T for r in range(RB)]
    one_bits = halo_bits(one_ref)
    agg_copy.wait()
    first = agg_ref[0]
    low, high = row_bits(count, agg_ref)
    zero = jnp.zeros((BS, BS), jnp.bfloat16)
    keep1 = (low == 0).astype(jnp.float32)
    keep2 = (high == 0).astype(jnp.float32)
    left[0, :BS, :BS] = turned[0].astype(jnp.bfloat16)
    left[0, :BS, BS:] = (turned[1] * keep1).astype(jnp.bfloat16)
    left[0, BS:, :BS] = zero
    left[0, BS:, BS:] = (turned[1] * (1 - keep1)).astype(jnp.bfloat16)
    left[1, :BS, :BS] = (turned[2] * keep2).astype(jnp.bfloat16)
    left[1, :BS, BS:] = zero
    left[1, BS:, :BS] = (turned[2] * (1 - keep2)).astype(jnp.bfloat16)
    left[1, BS:, BS:] = turned[3].astype(jnp.bfloat16)
    side_ref[...] = jnp.full((8, BS), (first + 1) & 7, jnp.int32).astype(jnp.float32)

    cols_copy.wait()
    for r in range(RB):
        for k in range(KT):
            place[r, (cols_ref[r, k] - first * RB) & (RB * count - 1)] = k
    odd = (first + 1) & 1
    inner = (1 - odd) * 2 * RB
    outer = odd * 2 * RB
    for copy in copies:
        copy.wait()
    for i in range(4):
        start = (RB if i < 2 else outer) + 2 * (i % 2)
        lhs = jnp.concatenate(
            [
                jnp.concatenate([tiles[r, place[r, start + c]] for c in range(2)], axis=1)
                for r in range(RB)
            ],
            axis=0,
        )
        n = 1 if i < 2 else 2 * odd
        add_pair(n, 2 * (i % 2), (low, high) if i < 2 else one_bits, lhs, weights.at[i], left, acc)
    for i in range(2):
        for r in range(RB):
            for c in range(2):
                tile = tiles[r, place[r, inner + 2 * i + c]]
                lhs_ref[i, r * BS : (r + 1) * BS, c * BS : (c + 1) * BS] = tile


def far_kernel(lhs_ref, left, near, side_ref, two_ref, out_ref, acc, weights):
    clear_weights(weights)
    for i in range(2):
        fill_weights(weights.at[i], two_ref, 2 * i)
    acc[...] = near[...]
    side = jnp.max(side_ref[...]).astype(jnp.int32)
    bits = halo_bits(two_ref)
    for i in range(2):
        add_pair(2 - 2 * (side & 1), 2 * i, bits, lhs_ref[i], weights.at[i], left, acc)
    for s in range(3):
        for j in range(5):
            block = acc[s, j].astype(jnp.bfloat16)
            for q in range(4):
                out_ref[q, s * 5 + j] = block[q * 32 : (q + 1) * 32, :]


def split_kernel(in_ref, up_ref, down_ref):
    up_ref[...] = in_ref[3, 10:]
    down_ref[...] = in_ref[0, :5]


def band_kernel(in_ref, out_hbm, open_ref, rows_ref, sems):
    def part(g, s, j):
        return in_ref[g, 5 * s + j].astype(jnp.float32)

    def block(c, j):
        terms = []
        if 1 <= j < 6:
            terms.append(part(c, 1, j - 1))
        if j < 5 and c > 0:
            terms.append(part(c - 1, 2, j))
        if j >= 2 and c < 3:
            terms.append(part(c + 1, 0, j - 2))
        total = terms[0] if terms else jnp.zeros((32, BS), jnp.float32)
        for term in terms[1:]:
            total = total + term
        return total

    copies = []
    for i, (c, js) in enumerate(((1, (0, 7)), (2, (0, 7)), (0, (5, 7)), (3, (0, 2)))):
        for j in range(*js):
            rows_ref[c, j] = block(c, j)
        here = pl.ds(js[0], js[1] - js[0])
        copies.append(pltpu.make_async_copy(rows_ref.at[c, here], out_hbm.at[c, here], sems.at[i]))
        copies[-1].start()
    for j in range(5):
        open_ref[0, j] = block(0, j)
        open_ref[1, j] = block(3, j + 2)
    for copy in copies:
        copy.wait()


def finish_kernel(open_ref, up_ref, down_ref, band_hbm, out_hbm, rows_ref, sems):
    del band_hbm
    copies = []
    for i, (got_ref, c, first) in enumerate(((up_ref, 0, 0), (down_ref, 3, 2))):
        rows_ref[i] = open_ref[i] + got_ref[...].astype(jnp.float32)
        copies.append(pltpu.make_async_copy(rows_ref.at[i], out_hbm.at[c, pl.ds(first, 5)], sems.at[i]))
        copies[-1].start()
    for copy in copies:
        copy.wait()


def shards(a_tiles, a_cols, p_tiles, p_agg):
    axes = ("rows", "grp")
    count = lax.axis_size(axes)
    params = pltpu.CompilerParams(vmem_limit_bytes=LIMIT)
    a_tiles, a_cols, p_tiles, p_agg = (
        pltpu.with_memory_space_constraint(x, pltpu.HBM) for x in (a_tiles, a_cols, p_tiles, p_agg)
    )
    packed = pl.pallas_call(
        functools.partial(pack_kernel, count),
        out_shape=jax.ShapeDtypeStruct((HALO, BS), jnp.bfloat16),
        in_specs=[HBM, HBM],
        out_specs=VMEM,
        scratch_shapes=[
            pltpu.SMEM((RB,), jnp.int32),
            pltpu.SemaphoreType.DMA,
            pltpu.SemaphoreType.DMA((RB,)),
        ],
        compiler_params=params,
        name="pack",
    )(p_agg, p_tiles)
    one = lax.ppermute(packed, axes, [(i, (i + 1 if i % 2 else i - 1) % count) for i in range(count)])
    two = lax.ppermute(packed, axes, [(i, i ^ 1) for i in range(count)])
    lhs, left, near, side = pl.pallas_call(
        functools.partial(near_kernel, count),
        out_shape=(
            jax.ShapeDtypeStruct((2, RB * BS, 2 * BS), jnp.bfloat16),
            jax.ShapeDtypeStruct((2, 2 * BS, 2 * BS), jnp.bfloat16),
            jax.ShapeDtypeStruct((3, 5, BS, BS), jnp.float32),
            jax.ShapeDtypeStruct((8, BS), jnp.float32),
        ),
        in_specs=[HBM, HBM, HBM, VMEM, VMEM],
        out_specs=(VMEM, VMEM, VMEM, VMEM),
        scratch_shapes=[
            pltpu.SMEM((RB, KT), jnp.int32),
            pltpu.SMEM((RB,), jnp.int32),
            pltpu.SMEM((RB, KT), jnp.int32),
            pltpu.VMEM((RB, KT, BS, BS), jnp.bfloat16),
            pltpu.VMEM((4, 2 * BS, 2 * BS), jnp.bfloat16),
            pltpu.SemaphoreType.DMA((2,)),
            pltpu.SemaphoreType.DMA((RB,)),
        ],
        compiler_params=params,
        cost_estimate=pl.CostEstimate(flops=2 * 10**8, bytes_accessed=4 * 10**6, transcendentals=0),
        name="near",
    )(a_cols, p_agg, a_tiles, packed, one)
    sums = pl.pallas_call(
        far_kernel,
        out_shape=jax.ShapeDtypeStruct((4, 15, 32, BS), jnp.bfloat16),
        in_specs=[VMEM] * 5,
        out_specs=VMEM,
        scratch_shapes=[
            pltpu.VMEM((3, 5, BS, BS), jnp.float32),
            pltpu.VMEM((2, 2 * BS, 2 * BS), jnp.bfloat16),
        ],
        compiler_params=params,
        name="far",
    )(lhs, left, near, side, two)
    parts = lax.all_to_all(sums, "grp", 0, 0, tiled=True)
    up, down = pl.pallas_call(
        split_kernel,
        out_shape=(jax.ShapeDtypeStruct((5, 32, BS), jnp.bfloat16),) * 2,
        in_specs=[VMEM],
        out_specs=(VMEM, VMEM),
        compiler_params=params,
        name="split",
    )(parts)
    got_up = lax.ppermute(up, axes, [(i, (i + 4) % count) for i in range(count)])
    got_down = lax.ppermute(down, axes, [(i, (i - 4) % count) for i in range(count)])
    band, unfinished = pl.pallas_call(
        band_kernel,
        out_shape=(
            jax.ShapeDtypeStruct((4, 7, 32, BS), jnp.float32),
            jax.ShapeDtypeStruct((2, 5, 32, BS), jnp.float32),
        ),
        in_specs=[VMEM],
        out_specs=(HBM, VMEM),
        scratch_shapes=[
            pltpu.VMEM((4, 7, 32, BS), jnp.float32),
            pltpu.SemaphoreType.DMA((4,)),
        ],
        compiler_params=params,
        cost_estimate=pl.CostEstimate(flops=10**7, bytes_accessed=2 * 10**6, transcendentals=0),
        name="band",
    )(parts)
    return pl.pallas_call(
        finish_kernel,
        out_shape=jax.ShapeDtypeStruct((4, 7, 32, BS), jnp.float32),
        in_specs=[VMEM, VMEM, VMEM, HBM],
        out_specs=HBM,
        input_output_aliases={3: 0},
        scratch_shapes=[
            pltpu.VMEM((2, 5, 32, BS), jnp.float32),
            pltpu.SemaphoreType.DMA((2,)),
        ],
        compiler_params=params,
        name="finish",
    )(unfinished, got_up, got_down, band)


def solution(mesh):
    in_specs = (
        P(("rows", "grp"), None, None, None),
        P(("rows", "grp"), None),
        P(("rows", "grp"), None, None),
        P(("rows", "grp")),
    )
    out_specs = P("rows", None, "grp", None)
    return jax.shard_map(shards, mesh=mesh, in_specs=in_specs, out_specs=out_specs, check_vma=False)
```

```python
import functools

import jax
import jax.numpy as jnp
from jax import lax
from jax.experimental import pallas as pl
from jax.experimental.pallas import tpu as pltpu
from jax.sharding import PartitionSpec as P

BS = 128
RB = 4
KT = 12
HALO = RB * BS + 16
HBM = pl.BlockSpec(memory_space=pltpu.HBM)
VMEM = pl.BlockSpec(memory_space=pltpu.VMEM)
LIMIT = 32 << 20


def row_bits(count, agg_ref):
    first = agg_ref[0]
    low = (agg_ref[1] - first) & (count - 1)
    high = ((agg_ref[2] - first) & (count - 1)) - 1
    return low, high


def pack_kernel(count, agg_hbm, p_hbm, out_ref, agg_ref, agg_sem, p_sem):
    agg_copy = pltpu.make_async_copy(agg_hbm, agg_ref, agg_sem)
    agg_copy.start()
    copies = [
        pltpu.make_async_copy(p_hbm.at[r], out_ref.at[pl.ds(r * BS, BS)], p_sem.at[r])
        for r in range(RB)
    ]
    for copy in copies:
        copy.start()
    agg_copy.wait()
    low, high = row_bits(count, agg_ref)
    half = lax.broadcasted_iota(jnp.int32, (16, BS), 0) < 8
    out_ref[RB * BS :, :] = jnp.where(half, low, high).astype(jnp.float32).astype(jnp.bfloat16)
    for copy in copies:
        copy.wait()


def extend_kernel(count, cols_hbm, agg_hbm, a_hbm, p_ref, out_ref, cols_ref, agg_ref, place, sems, a_sems):
    cols_copy = pltpu.make_async_copy(cols_hbm, cols_ref, sems.at[0])
    agg_copy = pltpu.make_async_copy(agg_hbm, agg_ref, sems.at[1])
    cols_copy.start()
    agg_copy.start()
    out_ref[:HALO, :] = p_ref[...]
    agg_copy.wait()
    cols_copy.wait()
    first = agg_ref[0]
    group_place = (first + 1) & 3
    top = group_place // 2 * 2
    base = (group_place & 1) * 2 * RB
    for r in range(2):
        for k in range(KT):
            place[r, (cols_ref[top + r, k] - first * RB) & (RB * count - 1)] = k
    copies = []
    for r in range(2):
        for c in range(RB):
            copies.append(
                pltpu.make_async_copy(
                    a_hbm.at[top + r, place[r, base + c]],
                    out_ref.at[pl.ds(HALO + (r * RB + c) * BS, BS)],
                    a_sems.at[r * RB + c],
                )
            )
            copies[-1].start()
    for copy in copies:
        copy.wait()


def halo_bits(ref):
    flags = ref[RB * BS : HALO, :].astype(jnp.float32)
    return (
        jnp.max(flags[:8, :]).astype(jnp.int32),
        jnp.max(flags[8:, :]).astype(jnp.int32),
    )


def fill_weights(w, tiles_ref, top):
    w[:BS, :BS] = tiles_ref[top * BS : (top + 1) * BS, :]
    w[BS:, BS:] = tiles_ref[(top + 1) * BS : (top + 2) * BS, :]


def clear_weights(weights):
    zero = jnp.zeros((BS, BS), jnp.bfloat16)
    for i in range(weights.shape[0]):
        weights[i, :BS, BS:] = zero
        weights[i, BS:, :BS] = zero


def add_pair(n, top, bits, lhs, w, left, acc):
    prod = jnp.dot(lhs, w[...], preferred_element_type=jnp.float32).astype(jnp.bfloat16)
    up = jnp.dot(left[0], prod[: 2 * BS], preferred_element_type=jnp.float32)
    down = jnp.dot(left[1], prod[2 * BS :], preferred_element_type=jnp.float32)
    slots = pair_slots(n, top, bits)
    for c in range(2):
        lanes = slice(c * BS, (c + 1) * BS)
        acc[0, slots[c]] += up[:BS, lanes]
        acc[1, slots[c]] += up[BS:, lanes] + down[:BS, lanes]
        acc[2, slots[c]] += down[BS:, lanes]


def pair_slots(n, top, bits):
    b1, b2 = bits
    return (n, n + b1) if top == 0 else (n + 1 + b2, n + 2)


def near_kernel(
    count, cols_hbm, agg_hbm, a_hbm, p_ref, two_ref, lhs_ref, left, acc, side_ref, edge_ref,
    cols_ref, agg_ref, place, tiles, weights, sems, a_sems,
):
    cols_copy = pltpu.make_async_copy(cols_hbm, cols_ref, sems.at[0])
    agg_copy = pltpu.make_async_copy(agg_hbm, agg_ref, sems.at[1])
    cols_copy.start()
    agg_copy.start()
    copies = [pltpu.make_async_copy(a_hbm.at[r], tiles.at[r], a_sems.at[r]) for r in range(RB)]
    for copy in copies:
        copy.start()
    clear_weights(weights)
    for i in range(4):
        fill_weights(weights.at[i], (p_ref, two_ref)[i // 2], 2 * (i % 2))
    acc[...] = jnp.zeros_like(acc)
    turned = [p_ref[r * BS : (r + 1) * BS, :].astype(jnp.float32).T for r in range(RB)]
    two_bits = halo_bits(two_ref)
    agg_copy.wait()
    first = agg_ref[0]
    low, high = row_bits(count, agg_ref)
    zero = jnp.zeros((BS, BS), jnp.bfloat16)
    keep1 = (low == 0).astype(jnp.float32)
    keep2 = (high == 0).astype(jnp.float32)
    left[0, :BS, :BS] = turned[0].astype(jnp.bfloat16)
    left[0, :BS, BS:] = (turned[1] * keep1).astype(jnp.bfloat16)
    left[0, BS:, :BS] = zero
    left[0, BS:, BS:] = (turned[1] * (1 - keep1)).astype(jnp.bfloat16)
    left[1, :BS, :BS] = (turned[2] * keep2).astype(jnp.bfloat16)
    left[1, :BS, BS:] = zero
    left[1, BS:, :BS] = (turned[2] * (1 - keep2)).astype(jnp.bfloat16)
    left[1, BS:, BS:] = turned[3].astype(jnp.bfloat16)
    side_ref[...] = jnp.full((8, BS), (first + 1) & 3, jnp.int32).astype(jnp.float32)

    cols_copy.wait()
    for r in range(RB):
        for k in range(KT):
            place[r, (cols_ref[r, k] - first * RB) & (RB * count - 1)] = k
    odd = (first + 1) & 1
    inner = (1 - odd) * 2 * RB
    outer = odd * 2 * RB
    for copy in copies:
        copy.wait()
    for i in range(4):
        start = (RB if i < 2 else inner) + 2 * (i % 2)
        lhs = jnp.concatenate(
            [
                jnp.concatenate([tiles[r, place[r, start + c]] for c in range(2)], axis=1)
                for r in range(RB)
            ],
            axis=0,
        )
        n = 1 if i < 2 else 2 * (1 - odd)
        add_pair(n, 2 * (i % 2), (low, high) if i < 2 else two_bits, lhs, weights.at[i], left, acc)
    for i in range(2):
        for r in range(RB):
            for c in range(2):
                tile = tiles[r, place[r, outer + 2 * i + c]]
                lhs_ref[i, r * BS : (r + 1) * BS, c * BS : (c + 1) * BS] = tile
    lower = side_ref[:1, :] < 2
    for j in range(5):
        edge_ref[j] = jnp.where(lower, acc[0, j], acc[2, j]).astype(jnp.bfloat16)


def rest_kernel(lhs_ref, left, near, side_ref, p_ref, one_ref, out_ref, acc, weights):
    clear_weights(weights)
    for i in range(2):
        fill_weights(weights.at[i], one_ref, 2 * i)
        fill_weights(weights.at[2 + i], p_ref, 2 * i)
    acc[...] = near[...]
    side = jnp.max(side_ref[...]).astype(jnp.int32)
    bits = halo_bits(one_ref)
    own_bits = halo_bits(p_ref)
    before, after = side == 0, side == 3
    top = jnp.where(before, 2 * BS, 0)
    keep = (
        jnp.where(before, bits[1], jnp.where(after, 1, 0)),
        jnp.where(before, 1, jnp.where(after, 1 - bits[0], 0)),
    )
    part = jnp.concatenate(
        [
            (
                one_ref[pl.ds(pl.multiple_of(top + r * BS, BS), BS), :].astype(jnp.float32).T
                * keep[r].astype(jnp.float32)
            ).astype(jnp.bfloat16)
            for r in range(2)
        ],
        axis=1,
    )
    for i in range(2):
        add_pair(2 * (side & 1), 2 * i, bits, lhs_ref[i], weights.at[i], left, acc)
        rows = [
            jnp.concatenate(
                [
                    one_ref[HALO + (r * RB + 2 * i + c) * BS : HALO + (r * RB + 2 * i + c + 1) * BS, :]
                    for c in range(2)
                ],
                axis=1,
            )
            for r in range(2)
        ]
        prod = jnp.dot(
            jnp.concatenate(rows, axis=0), weights[2 + i], preferred_element_type=jnp.float32
        ).astype(jnp.bfloat16)
        sums = jnp.dot(part, prod, preferred_element_type=jnp.float32)
        slots = pair_slots(1, 2 * i, own_bits)
        for c in range(2):
            acc[1, slots[c]] += sums[:, c * BS : (c + 1) * BS]
    for s in range(3):
        for j in range(5):
            block = acc[s, j].astype(jnp.bfloat16)
            for q in range(4):
                out_ref[q, s * 5 + j] = block[q * 32 : (q + 1) * 32, :]


def join_kernel(side_ref, got_ref, sums_ref, out_ref):
    for side, base in ((0, 0), (3, 10)):
        here = side_ref[:1, :] == side
        for j in range(5):
            for q in range(4):
                new = got_ref[j, q * 32 : (q + 1) * 32, :].astype(jnp.float32)
                old = sums_ref[q, base + j].astype(jnp.float32)
                out_ref[q, base + j] = jnp.where(here, new, old).astype(jnp.bfloat16)
    for q in range(4):
        out_ref[q, 5:10] = sums_ref[q, 5:10]


def band_kernel(in_ref, out_hbm, out_ref, sems):
    def part(g, s, j):
        return in_ref[g, 5 * s + j].astype(jnp.float32)

    copies = []
    for c in range(4):
        for j in range(7):
            terms = []
            if 1 <= j < 6:
                terms.append(part(c, 1, j - 1))
            if j < 5:
                terms.append(part(c - 1, 2, j) if c > 0 else part(3, 2, j))
            if j >= 2:
                terms.append(part(c + 1, 0, j - 2) if c < 3 else part(0, 0, j - 2))
            total = terms[0]
            for term in terms[1:]:
                total = total + term
            out_ref[c, j] = total
        copies.append(pltpu.make_async_copy(out_ref.at[c], out_hbm.at[c], sems.at[c]))
        copies[-1].start()
    for copy in copies:
        copy.wait()


def shards(a_tiles, a_cols, p_tiles, p_agg):
    axes = ("rows", "grp")
    count = lax.axis_size(axes)
    params = pltpu.CompilerParams(vmem_limit_bytes=LIMIT)
    a_tiles, a_cols, p_tiles, p_agg = (
        pltpu.with_memory_space_constraint(x, pltpu.HBM) for x in (a_tiles, a_cols, p_tiles, p_agg)
    )
    packed = pl.pallas_call(
        functools.partial(pack_kernel, count),
        out_shape=jax.ShapeDtypeStruct((HALO, BS), jnp.bfloat16),
        in_specs=[HBM, HBM],
        out_specs=VMEM,
        scratch_shapes=[
            pltpu.SMEM((RB,), jnp.int32),
            pltpu.SemaphoreType.DMA,
            pltpu.SemaphoreType.DMA((RB,)),
        ],
        compiler_params=params,
        name="pack",
    )(p_agg, p_tiles)
    two = lax.ppermute(packed, axes, [(i, i ^ 1) for i in range(count)])
    wide = pl.pallas_call(
        functools.partial(extend_kernel, count),
        out_shape=jax.ShapeDtypeStruct((HALO + 2 * RB * BS, BS), jnp.bfloat16),
        in_specs=[HBM, HBM, HBM, VMEM],
        out_specs=VMEM,
        scratch_shapes=[
            pltpu.SMEM((RB, KT), jnp.int32),
            pltpu.SMEM((RB,), jnp.int32),
            pltpu.SMEM((2, KT), jnp.int32),
            pltpu.SemaphoreType.DMA((2,)),
            pltpu.SemaphoreType.DMA((2 * RB,)),
        ],
        compiler_params=params,
        name="extend",
    )(a_cols, p_agg, a_tiles, packed)
    one = lax.ppermute(wide, axes, [(i, (i + 1 if i % 2 else i - 1) % count) for i in range(count)])
    lhs, left, near, side, edge = pl.pallas_call(
        functools.partial(near_kernel, count),
        out_shape=(
            jax.ShapeDtypeStruct((2, RB * BS, 2 * BS), jnp.bfloat16),
            jax.ShapeDtypeStruct((2, 2 * BS, 2 * BS), jnp.bfloat16),
            jax.ShapeDtypeStruct((3, 5, BS, BS), jnp.float32),
            jax.ShapeDtypeStruct((8, BS), jnp.float32),
            jax.ShapeDtypeStruct((5, BS, BS), jnp.bfloat16),
        ),
        in_specs=[HBM, HBM, HBM, VMEM, VMEM],
        out_specs=(VMEM, VMEM, VMEM, VMEM, VMEM),
        scratch_shapes=[
            pltpu.SMEM((RB, KT), jnp.int32),
            pltpu.SMEM((RB,), jnp.int32),
            pltpu.SMEM((RB, KT), jnp.int32),
            pltpu.VMEM((RB, KT, BS, BS), jnp.bfloat16),
            pltpu.VMEM((4, 2 * BS, 2 * BS), jnp.bfloat16),
            pltpu.SemaphoreType.DMA((2,)),
            pltpu.SemaphoreType.DMA((RB,)),
        ],
        compiler_params=params,
        cost_estimate=pl.CostEstimate(flops=2 * 10**10, bytes_accessed=10**8, transcendentals=0),
        name="near",
    )(a_cols, p_agg, a_tiles, packed, two)
    cross = []
    for i in range(0, count, 4):
        cross.append((i, (i - 4) % count))
        cross.append((i + 3, (i + 7) % count))
    got = lax.ppermute(edge, axes, cross)
    sums = pl.pallas_call(
        rest_kernel,
        out_shape=jax.ShapeDtypeStruct((4, 15, 32, BS), jnp.bfloat16),
        in_specs=[VMEM] * 6,
        out_specs=VMEM,
        scratch_shapes=[
            pltpu.VMEM((3, 5, BS, BS), jnp.float32),
            pltpu.VMEM((4, 2 * BS, 2 * BS), jnp.bfloat16),
        ],
        compiler_params=params,
        cost_estimate=pl.CostEstimate(flops=2 * 10**8, bytes_accessed=3 * 10**6, transcendentals=0),
        name="rest",
    )(lhs, left, near, side, packed, one)
    joined = pl.pallas_call(
        join_kernel,
        out_shape=jax.ShapeDtypeStruct((4, 15, 32, BS), jnp.bfloat16),
        in_specs=[VMEM, VMEM, VMEM],
        out_specs=VMEM,
        compiler_params=params,
        name="join",
    )(side, got, sums)
    parts = lax.all_to_all(joined, "grp", 0, 0, tiled=True)
    return pl.pallas_call(
        band_kernel,
        out_shape=jax.ShapeDtypeStruct((4, 7, 32, BS), jnp.float32),
        in_specs=[VMEM],
        out_specs=HBM,
        scratch_shapes=[
            pltpu.VMEM((4, 7, 32, BS), jnp.float32),
            pltpu.SemaphoreType.DMA((4,)),
        ],
        compiler_params=params,
        name="band",
    )(parts)


def solution(mesh):
    in_specs = (
        P(("rows", "grp"), None, None, None),
        P(("rows", "grp"), None),
        P(("rows", "grp"), None, None),
        P(("rows", "grp")),
    )
    out_specs = P("rows", None, "grp", None)
    return jax.shard_map(shards, mesh=mesh, in_specs=in_specs, out_specs=out_specs, check_vma=False)
```

```python
import functools

import jax
import jax.numpy as jnp
from jax import lax
from jax.experimental import pallas as pl
from jax.experimental.pallas import tpu as pltpu
from jax.sharding import PartitionSpec as P

BS = 128
RB = 4
KT = 12
HALO = RB * BS + 16
HBM = pl.BlockSpec(memory_space=pltpu.HBM)
VMEM = pl.BlockSpec(memory_space=pltpu.VMEM)
LIMIT = 32 << 20


def row_bits(count, agg_ref):
    first = agg_ref[0]
    low = (agg_ref[1] - first) & (count - 1)
    high = ((agg_ref[2] - first) & (count - 1)) - 1
    return low, high


def pack_kernel(count, agg_hbm, p_hbm, out_ref, agg_ref, agg_sem, p_sem):
    agg_copy = pltpu.make_async_copy(agg_hbm, agg_ref, agg_sem)
    agg_copy.start()
    copies = [
        pltpu.make_async_copy(p_hbm.at[r], out_ref.at[pl.ds(r * BS, BS)], p_sem.at[r])
        for r in range(RB)
    ]
    for copy in copies:
        copy.start()
    agg_copy.wait()
    low, high = row_bits(count, agg_ref)
    half = lax.broadcasted_iota(jnp.int32, (16, BS), 0) < 8
    out_ref[RB * BS :, :] = jnp.where(half, low, high).astype(jnp.float32).astype(jnp.bfloat16)
    for copy in copies:
        copy.wait()


def extend_kernel(
    count, cols_hbm, agg_hbm, a_hbm, p_ref, out_ref, lhs_ref, left, side_ref,
    cols_ref, agg_ref, place, tiles, sems, a_sems,
):
    cols_copy = pltpu.make_async_copy(cols_hbm, cols_ref, sems.at[0])
    agg_copy = pltpu.make_async_copy(agg_hbm, agg_ref, sems.at[1])
    cols_copy.start()
    agg_copy.start()
    copies = [
        pltpu.make_async_copy(a_hbm.at[r, pl.ds(6 * h, 6)], tiles.at[r, pl.ds(6 * h, 6)], a_sems.at[r, h])
        for r in range(RB)
        for h in range(2)
    ]
    for copy in copies:
        copy.start()
    out_ref[:HALO, :] = p_ref[...]
    agg_copy.wait()
    first = agg_ref[0]
    low, high = row_bits(count, agg_ref)
    turned = [p_ref[r * BS : (r + 1) * BS, :].astype(jnp.float32).T for r in range(RB)]
    zero = jnp.zeros((BS, BS), jnp.bfloat16)
    keep1 = (low == 0).astype(jnp.float32)
    keep2 = (high == 0).astype(jnp.float32)
    left[0, :BS, :BS] = turned[0].astype(jnp.bfloat16)
    left[0, :BS, BS:] = (turned[1] * keep1).astype(jnp.bfloat16)
    left[0, BS:, :BS] = zero
    left[0, BS:, BS:] = (turned[1] * (1 - keep1)).astype(jnp.bfloat16)
    left[1, :BS, :BS] = (turned[2] * keep2).astype(jnp.bfloat16)
    left[1, :BS, BS:] = zero
    left[1, BS:, :BS] = (turned[2] * (1 - keep2)).astype(jnp.bfloat16)
    left[1, BS:, BS:] = turned[3].astype(jnp.bfloat16)
    group_place = (first + 1) & 3
    side_ref[...] = jnp.full((8, BS), group_place, jnp.int32).astype(jnp.float32)
    cols_copy.wait()
    for r in range(RB):
        for k in range(KT):
            place[r, (cols_ref[r, k] - first * RB) & (RB * count - 1)] = k
    odd = (first + 1) & 1
    inner = (1 - odd) * 2 * RB
    outer = odd * 2 * RB
    for copy in copies:
        copy.wait()
    for i in range(6):
        start = (RB, inner, outer)[i // 2] + 2 * (i % 2)
        for r in range(RB):
            for c in range(2):
                lhs_ref[i, r * BS : (r + 1) * BS, c * BS : (c + 1) * BS] = tiles[r, place[r, start + c]]
    top = group_place // 2 * 2
    for r in range(2):
        for c in range(RB):
            to = HALO + (r * RB + c) * BS
            out_ref[to : to + BS, :] = tiles[top + r, place[top + r, outer + c]]


def halo_bits(ref):
    flags = ref[RB * BS : HALO, :].astype(jnp.float32)
    return (
        jnp.max(flags[:8, :]).astype(jnp.int32),
        jnp.max(flags[8:, :]).astype(jnp.int32),
    )


def fill_weights(w, tiles_ref, top):
    w[:BS, :BS] = tiles_ref[top * BS : (top + 1) * BS, :]
    w[BS:, BS:] = tiles_ref[(top + 1) * BS : (top + 2) * BS, :]


def clear_weights(weights):
    zero = jnp.zeros((BS, BS), jnp.bfloat16)
    for i in range(weights.shape[0]):
        weights[i, :BS, BS:] = zero
        weights[i, BS:, :BS] = zero


def add_pair(n, top, bits, lhs, w, left, acc):
    prod = jnp.dot(lhs, w[...], preferred_element_type=jnp.float32).astype(jnp.bfloat16)
    up = jnp.dot(left[0], prod[: 2 * BS], preferred_element_type=jnp.float32)
    down = jnp.dot(left[1], prod[2 * BS :], preferred_element_type=jnp.float32)
    slots = pair_slots(n, top, bits)
    for c in range(2):
        lanes = slice(c * BS, (c + 1) * BS)
        acc[0, slots[c]] += up[:BS, lanes]
        acc[1, slots[c]] += up[BS:, lanes] + down[:BS, lanes]
        acc[2, slots[c]] += down[BS:, lanes]


def pair_slots(n, top, bits):
    b1, b2 = bits
    return (n, n + b1) if top == 0 else (n + 1 + b2, n + 2)


def near_kernel(lhs_ref, left, side_ref, p_ref, two_ref, acc, edge_ref, weights):
    clear_weights(weights)
    for i in range(4):
        fill_weights(weights.at[i], (p_ref, two_ref)[i // 2], 2 * (i % 2))
    acc[...] = jnp.zeros_like(acc)
    side = jnp.max(side_ref[...]).astype(jnp.int32)
    own_bits, two_bits = halo_bits(p_ref), halo_bits(two_ref)
    for i in range(4):
        n = 1 if i < 2 else 2 - 2 * (side & 1)
        add_pair(n, 2 * (i % 2), own_bits if i < 2 else two_bits, lhs_ref[i], weights.at[i], left, acc)
    lower = side_ref[:1, :] < 2
    for j in range(4):
        edge_ref[j] = jnp.where(lower, acc[0, j + 1], acc[2, j]).astype(jnp.bfloat16)


def rest_kernel(lhs_ref, left, near, side_ref, p_ref, one_ref, out_ref, acc, weights):
    clear_weights(weights)
    for i in range(2):
        fill_weights(weights.at[i], one_ref, 2 * i)
        fill_weights(weights.at[2 + i], p_ref, 2 * i)
    acc[...] = near[...]
    side = jnp.max(side_ref[...]).astype(jnp.int32)
    bits = halo_bits(one_ref)
    own_bits = halo_bits(p_ref)
    before, after = side == 0, side == 3
    top = jnp.where(before, 2 * BS, 0)
    keep = (
        jnp.where(before, bits[1], jnp.where(after, 1, 0)),
        jnp.where(before, 1, jnp.where(after, 1 - bits[0], 0)),
    )
    part = jnp.concatenate(
        [
            (
                one_ref[pl.ds(pl.multiple_of(top + r * BS, BS), BS), :].astype(jnp.float32).T
                * keep[r].astype(jnp.float32)
            ).astype(jnp.bfloat16)
            for r in range(2)
        ],
        axis=1,
    )
    for i in range(2):
        add_pair(2 * (side & 1), 2 * i, bits, lhs_ref[4 + i], weights.at[i], left, acc)
        rows = [
            jnp.concatenate(
                [
                    one_ref[HALO + (r * RB + 2 * i + c) * BS : HALO + (r * RB + 2 * i + c + 1) * BS, :]
                    for c in range(2)
                ],
                axis=1,
            )
            for r in range(2)
        ]
        prod = jnp.dot(
            jnp.concatenate(rows, axis=0), weights[2 + i], preferred_element_type=jnp.float32
        ).astype(jnp.bfloat16)
        sums = jnp.dot(part, prod, preferred_element_type=jnp.float32)
        slots = pair_slots(1, 2 * i, own_bits)
        for c in range(2):
            acc[1, slots[c]] += sums[:, c * BS : (c + 1) * BS]
    for s in range(3):
        for j in range(5):
            block = acc[s, j].astype(jnp.bfloat16)
            for q in range(4):
                out_ref[q, s * 5 + j] = block[q * 32 : (q + 1) * 32, :]


def join_kernel(side_ref, got_ref, sums_ref, out_ref):
    for side, base, shift in ((0, 0, 1), (3, 10, 0)):
        here = side_ref[:1, :] == side
        for j in range(5):
            for q in range(4):
                old = sums_ref[q, base + j].astype(jnp.float32)
                if 0 <= j - shift < 4:
                    new = got_ref[j - shift, q * 32 : (q + 1) * 32, :].astype(jnp.float32)
                else:
                    new = jnp.zeros_like(old)
                out_ref[q, base + j] = jnp.where(here, new, old).astype(jnp.bfloat16)
    for q in range(4):
        out_ref[q, 5:10] = sums_ref[q, 5:10]


def band_kernel(in_ref, out_hbm, out_ref, sems):
    def part(g, s, j):
        return in_ref[g, 5 * s + j].astype(jnp.float32)

    copies = []
    for c in range(4):
        for j in range(7):
            terms = []
            if 1 <= j < 6:
                terms.append(part(c, 1, j - 1))
            if j < 5:
                terms.append(part(c - 1, 2, j) if c > 0 else part(3, 2, j))
            if j >= 2:
                terms.append(part(c + 1, 0, j - 2) if c < 3 else part(0, 0, j - 2))
            total = terms[0]
            for term in terms[1:]:
                total = total + term
            out_ref[c, j] = total
            if j in (2, 6):
                here = pl.ds(0, 3) if j == 2 else pl.ds(3, 4)
                sem = sems.at[2 * c + j // 6]
                copies.append(pltpu.make_async_copy(out_ref.at[c, here], out_hbm.at[c, here], sem))
                copies[-1].start()
    for copy in copies:
        copy.wait()


def shards(a_tiles, a_cols, p_tiles, p_agg):
    axes = ("rows", "grp")
    count = lax.axis_size(axes)
    params = pltpu.CompilerParams(vmem_limit_bytes=LIMIT)
    a_tiles, a_cols, p_tiles, p_agg = (
        pltpu.with_memory_space_constraint(x, pltpu.HBM) for x in (a_tiles, a_cols, p_tiles, p_agg)
    )
    packed = pl.pallas_call(
        functools.partial(pack_kernel, count),
        out_shape=jax.ShapeDtypeStruct((HALO, BS), jnp.bfloat16),
        in_specs=[HBM, HBM],
        out_specs=VMEM,
        scratch_shapes=[
            pltpu.SMEM((RB,), jnp.int32),
            pltpu.SemaphoreType.DMA,
            pltpu.SemaphoreType.DMA((RB,)),
        ],
        compiler_params=params,
        name="pack",
    )(p_agg, p_tiles)
    two = lax.ppermute(packed, axes, [(i, i ^ 1) for i in range(count)])
    wide, lhs, left, side = pl.pallas_call(
        functools.partial(extend_kernel, count),
        out_shape=(
            jax.ShapeDtypeStruct((HALO + 2 * RB * BS, BS), jnp.bfloat16),
            jax.ShapeDtypeStruct((6, RB * BS, 2 * BS), jnp.bfloat16),
            jax.ShapeDtypeStruct((2, 2 * BS, 2 * BS), jnp.bfloat16),
            jax.ShapeDtypeStruct((8, BS), jnp.float32),
        ),
        in_specs=[HBM, HBM, HBM, VMEM],
        out_specs=(VMEM, VMEM, VMEM, VMEM),
        scratch_shapes=[
            pltpu.SMEM((RB, KT), jnp.int32),
            pltpu.SMEM((RB,), jnp.int32),
            pltpu.SMEM((RB, KT), jnp.int32),
            pltpu.VMEM((RB, KT, BS, BS), jnp.bfloat16),
            pltpu.SemaphoreType.DMA((2,)),
            pltpu.SemaphoreType.DMA((RB, 2)),
        ],
        compiler_params=params,
        name="extend",
    )(a_cols, p_agg, a_tiles, packed)
    one = lax.ppermute(wide, axes, [(i, (i + 1 if i % 2 else i - 1) % count) for i in range(count)])
    near, edge = pl.pallas_call(
        near_kernel,
        out_shape=(
            jax.ShapeDtypeStruct((3, 5, BS, BS), jnp.float32),
            jax.ShapeDtypeStruct((4, BS, BS), jnp.bfloat16),
        ),
        in_specs=[VMEM] * 5,
        out_specs=(VMEM, VMEM),
        scratch_shapes=[pltpu.VMEM((4, 2 * BS, 2 * BS), jnp.bfloat16)],
        compiler_params=params,
        cost_estimate=pl.CostEstimate(flops=2 * 10**10, bytes_accessed=10**8, transcendentals=0),
        name="near",
    )(lhs, left, side, packed, two)
    cross = []
    for i in range(0, count, 4):
        cross.append((i, (i - 4) % count))
        cross.append((i + 3, (i + 7) % count))
    got = lax.ppermute(edge, axes, cross)
    sums = pl.pallas_call(
        rest_kernel,
        out_shape=jax.ShapeDtypeStruct((4, 15, 32, BS), jnp.bfloat16),
        in_specs=[VMEM] * 6,
        out_specs=VMEM,
        scratch_shapes=[
            pltpu.VMEM((3, 5, BS, BS), jnp.float32),
            pltpu.VMEM((4, 2 * BS, 2 * BS), jnp.bfloat16),
        ],
        compiler_params=params,
        cost_estimate=pl.CostEstimate(flops=2 * 10**8, bytes_accessed=3 * 10**6, transcendentals=0),
        name="rest",
    )(lhs, left, near, side, packed, one)
    joined = pl.pallas_call(
        join_kernel,
        out_shape=jax.ShapeDtypeStruct((4, 15, 32, BS), jnp.bfloat16),
        in_specs=[VMEM, VMEM, VMEM],
        out_specs=VMEM,
        compiler_params=params,
        name="join",
    )(side, got, sums)
    parts = lax.all_to_all(joined, "grp", 0, 0, tiled=True)
    return pl.pallas_call(
        band_kernel,
        out_shape=jax.ShapeDtypeStruct((4, 7, 32, BS), jnp.float32),
        in_specs=[VMEM],
        out_specs=HBM,
        scratch_shapes=[
            pltpu.VMEM((4, 7, 32, BS), jnp.float32),
            pltpu.SemaphoreType.DMA((8,)),
        ],
        compiler_params=params,
        name="band",
    )(parts)


def solution(mesh):
    in_specs = (
        P(("rows", "grp"), None, None, None),
        P(("rows", "grp"), None),
        P(("rows", "grp"), None, None),
        P(("rows", "grp")),
    )
    out_specs = P("rows", None, "grp", None)
    return jax.shard_map(shards, mesh=mesh, in_specs=in_specs, out_specs=out_specs, check_vma=False)
```

```python
import functools

import jax
import jax.numpy as jnp
from jax import lax
from jax.experimental import pallas as pl
from jax.experimental.pallas import tpu as pltpu
from jax.sharding import PartitionSpec as P

BS = 128
RB = 4
KT = 12
HALO = RB * BS + 16
HBM = pl.BlockSpec(memory_space=pltpu.HBM)
VMEM = pl.BlockSpec(memory_space=pltpu.VMEM)
LIMIT = 32 << 20


def row_bits(count, agg_ref):
    first = agg_ref[0]
    low = (agg_ref[1] - first) & (count - 1)
    high = ((agg_ref[2] - first) & (count - 1)) - 1
    return low, high


def pack_kernel(count, agg_hbm, p_hbm, out_ref, agg_ref, agg_sem, p_sem):
    agg_copy = pltpu.make_async_copy(agg_hbm, agg_ref, agg_sem)
    agg_copy.start()
    copies = [
        pltpu.make_async_copy(p_hbm.at[r], out_ref.at[pl.ds(r * BS, BS)], p_sem.at[r])
        for r in range(RB)
    ]
    for copy in copies:
        copy.start()
    agg_copy.wait()
    low, high = row_bits(count, agg_ref)
    half = lax.broadcasted_iota(jnp.int32, (16, BS), 0) < 8
    out_ref[RB * BS :, :] = jnp.where(half, low, high).astype(jnp.float32).astype(jnp.bfloat16)
    for copy in copies:
        copy.wait()


def extend_kernel(
    count, cols_hbm, agg_hbm, a_hbm, p_ref, out_ref, lhs_ref, left, side_ref,
    cols_ref, agg_ref, place, tiles, sems, a_sems,
):
    cols_copy = pltpu.make_async_copy(cols_hbm, cols_ref, sems.at[0])
    agg_copy = pltpu.make_async_copy(agg_hbm, agg_ref, sems.at[1])
    cols_copy.start()
    agg_copy.start()
    copies = [
        pltpu.make_async_copy(a_hbm.at[r, pl.ds(6 * h, 6)], tiles.at[r, pl.ds(6 * h, 6)], a_sems.at[r, h])
        for r in range(RB)
        for h in range(2)
    ]
    for copy in copies:
        copy.start()
    out_ref[:HALO, :] = p_ref[...]
    agg_copy.wait()
    first = agg_ref[0]
    low, high = row_bits(count, agg_ref)
    turned = [p_ref[r * BS : (r + 1) * BS, :].astype(jnp.float32).T for r in range(RB)]
    zero = jnp.zeros((BS, BS), jnp.bfloat16)
    keep1 = (low == 0).astype(jnp.float32)
    keep2 = (high == 0).astype(jnp.float32)
    left[0, :BS, :BS] = turned[0].astype(jnp.bfloat16)
    left[0, :BS, BS:] = (turned[1] * keep1).astype(jnp.bfloat16)
    left[0, BS:, :BS] = zero
    left[0, BS:, BS:] = (turned[1] * (1 - keep1)).astype(jnp.bfloat16)
    left[1, :BS, :BS] = (turned[2] * keep2).astype(jnp.bfloat16)
    left[1, :BS, BS:] = zero
    left[1, BS:, :BS] = (turned[2] * (1 - keep2)).astype(jnp.bfloat16)
    left[1, BS:, BS:] = turned[3].astype(jnp.bfloat16)
    group_place = (first + 1) & 3
    side_ref[...] = jnp.full((8, BS), group_place, jnp.int32).astype(jnp.float32)
    cols_copy.wait()
    for r in range(RB):
        for k in range(KT):
            place[r, (cols_ref[r, k] - first * RB) & (RB * count - 1)] = k
    odd = (first + 1) & 1
    inner = (1 - odd) * 2 * RB
    outer = odd * 2 * RB
    for copy in copies:
        copy.wait()
    for i in range(6):
        start = (RB, inner, outer)[i // 2] + 2 * (i % 2)
        for r in range(RB):
            for c in range(2):
                lhs_ref[i, r * BS : (r + 1) * BS, c * BS : (c + 1) * BS] = tiles[r, place[r, start + c]]
    h = group_place // 2
    border = jnp.where((group_place == 0) | (group_place == 3), 1, 0).astype(jnp.float32)
    part = left[h, pl.ds(pl.multiple_of(h * BS, BS), BS), :]
    rows = pl.ds(pl.multiple_of(h * 2 * BS, 2 * BS), 2 * BS)
    for i in range(2):
        both = jnp.dot(part, lhs_ref[4 + i, rows, :], preferred_element_type=jnp.float32) * border
        for c in range(2):
            to = HALO + (2 * i + c) * BS
            out_ref[to : to + BS, :] = both[:, c * BS : (c + 1) * BS].astype(jnp.bfloat16)


def halo_bits(ref):
    flags = ref[RB * BS : HALO, :].astype(jnp.float32)
    return (
        jnp.max(flags[:8, :]).astype(jnp.int32),
        jnp.max(flags[8:, :]).astype(jnp.int32),
    )


def fill_weights(w, tiles_ref, top):
    w[:BS, :BS] = tiles_ref[top * BS : (top + 1) * BS, :]
    w[BS:, BS:] = tiles_ref[(top + 1) * BS : (top + 2) * BS, :]


def clear_weights(weights):
    zero = jnp.zeros((BS, BS), jnp.bfloat16)
    for i in range(weights.shape[0]):
        weights[i, :BS, BS:] = zero
        weights[i, BS:, :BS] = zero


def add_pair(n, top, bits, lhs, w, left, acc):
    prod = jnp.dot(lhs, w[...], preferred_element_type=jnp.float32).astype(jnp.bfloat16)
    up = jnp.dot(left[0], prod[: 2 * BS], preferred_element_type=jnp.float32)
    down = jnp.dot(left[1], prod[2 * BS :], preferred_element_type=jnp.float32)
    slots = pair_slots(n, top, bits)
    for c in range(2):
        lanes = slice(c * BS, (c + 1) * BS)
        acc[0, slots[c]] += up[:BS, lanes]
        acc[1, slots[c]] += up[BS:, lanes] + down[:BS, lanes]
        acc[2, slots[c]] += down[BS:, lanes]


def pair_slots(n, top, bits):
    b1, b2 = bits
    return (n, n + b1) if top == 0 else (n + 1 + b2, n + 2)


def near_kernel(lhs_ref, left, side_ref, p_ref, two_ref, acc, edge_ref, weights):
    clear_weights(weights)
    for i in range(4):
        fill_weights(weights.at[i], (p_ref, two_ref)[i // 2], 2 * (i % 2))
    acc[...] = jnp.zeros_like(acc)
    side = jnp.max(side_ref[...]).astype(jnp.int32)
    own_bits, two_bits = halo_bits(p_ref), halo_bits(two_ref)
    for i in range(4):
        n = 1 if i < 2 else 2 - 2 * (side & 1)
        add_pair(n, 2 * (i % 2), own_bits if i < 2 else two_bits, lhs_ref[i], weights.at[i], left, acc)
    lower = side_ref[:1, :] < 2
    for j in range(4):
        edge_ref[j] = jnp.where(lower, acc[0, j + 1], acc[2, j]).astype(jnp.bfloat16)


def rest_kernel(lhs_ref, left, near, side_ref, p_ref, one_ref, out_ref, acc, weights):
    clear_weights(weights)
    for i in range(2):
        fill_weights(weights.at[i], one_ref, 2 * i)
        fill_weights(weights.at[2 + i], p_ref, 2 * i)
    acc[...] = near[...]
    side = jnp.max(side_ref[...]).astype(jnp.int32)
    bits = halo_bits(one_ref)
    own_bits = halo_bits(p_ref)
    for i in range(2):
        add_pair(2 * (side & 1), 2 * i, bits, lhs_ref[4 + i], weights.at[i], left, acc)
        both = jnp.concatenate(
            [one_ref[HALO + (2 * i + c) * BS : HALO + (2 * i + c + 1) * BS, :] for c in range(2)], axis=1
        )
        sums = jnp.dot(both, weights[2 + i], preferred_element_type=jnp.float32)
        slots = pair_slots(1, 2 * i, own_bits)
        for c in range(2):
            acc[1, slots[c]] += sums[:, c * BS : (c + 1) * BS]
    for s in range(3):
        for j in range(5):
            block = acc[s, j].astype(jnp.bfloat16)
            for q in range(4):
                out_ref[q, s * 5 + j] = block[q * 32 : (q + 1) * 32, :]


def join_kernel(side_ref, got_ref, sums_ref, out_ref):
    for side, base, shift in ((0, 0, 1), (3, 10, 0)):
        here = side_ref[:1, :] == side
        for j in range(5):
            for q in range(4):
                old = sums_ref[q, base + j].astype(jnp.float32)
                if 0 <= j - shift < 4:
                    new = got_ref[j - shift, q * 32 : (q + 1) * 32, :].astype(jnp.float32)
                else:
                    new = jnp.zeros_like(old)
                out_ref[q, base + j] = jnp.where(here, new, old).astype(jnp.bfloat16)
    for q in range(4):
        out_ref[q, 5:10] = sums_ref[q, 5:10]


def band_kernel(in_ref, out_hbm, out_ref, sems):
    def part(g, s, j):
        return in_ref[g, 5 * s + j].astype(jnp.float32)

    copies = []
    for c in range(4):
        for j in range(7):
            terms = []
            if 1 <= j < 6:
                terms.append(part(c, 1, j - 1))
            if j < 5:
                terms.append(part(c - 1, 2, j) if c > 0 else part(3, 2, j))
            if j >= 2:
                terms.append(part(c + 1, 0, j - 2) if c < 3 else part(0, 0, j - 2))
            total = terms[0]
            for term in terms[1:]:
                total = total + term
            out_ref[c, j] = total
            if j in (2, 6):
                here = pl.ds(0, 3) if j == 2 else pl.ds(3, 4)
                sem = sems.at[2 * c + j // 6]
                copies.append(pltpu.make_async_copy(out_ref.at[c, here], out_hbm.at[c, here], sem))
                copies[-1].start()
    for copy in copies:
        copy.wait()


def shards(a_tiles, a_cols, p_tiles, p_agg):
    axes = ("rows", "grp")
    count = lax.axis_size(axes)
    params = pltpu.CompilerParams(vmem_limit_bytes=LIMIT)
    a_tiles, a_cols, p_tiles, p_agg = (
        pltpu.with_memory_space_constraint(x, pltpu.HBM) for x in (a_tiles, a_cols, p_tiles, p_agg)
    )
    packed = pl.pallas_call(
        functools.partial(pack_kernel, count),
        out_shape=jax.ShapeDtypeStruct((HALO, BS), jnp.bfloat16),
        in_specs=[HBM, HBM],
        out_specs=VMEM,
        scratch_shapes=[
            pltpu.SMEM((RB,), jnp.int32),
            pltpu.SemaphoreType.DMA,
            pltpu.SemaphoreType.DMA((RB,)),
        ],
        compiler_params=params,
        name="pack",
    )(p_agg, p_tiles)
    two = lax.ppermute(packed, axes, [(i, i ^ 1) for i in range(count)])
    wide, lhs, left, side = pl.pallas_call(
        functools.partial(extend_kernel, count),
        out_shape=(
            jax.ShapeDtypeStruct((HALO + RB * BS, BS), jnp.bfloat16),
            jax.ShapeDtypeStruct((6, RB * BS, 2 * BS), jnp.bfloat16),
            jax.ShapeDtypeStruct((2, 2 * BS, 2 * BS), jnp.bfloat16),
            jax.ShapeDtypeStruct((8, BS), jnp.float32),
        ),
        in_specs=[HBM, HBM, HBM, VMEM],
        out_specs=(VMEM, VMEM, VMEM, VMEM),
        scratch_shapes=[
            pltpu.SMEM((RB, KT), jnp.int32),
            pltpu.SMEM((RB,), jnp.int32),
            pltpu.SMEM((RB, KT), jnp.int32),
            pltpu.VMEM((RB, KT, BS, BS), jnp.bfloat16),
            pltpu.SemaphoreType.DMA((2,)),
            pltpu.SemaphoreType.DMA((RB, 2)),
        ],
        compiler_params=params,
        name="extend",
    )(a_cols, p_agg, a_tiles, packed)
    one = lax.ppermute(wide, axes, [(i, (i + 1 if i % 2 else i - 1) % count) for i in range(count)])
    near, edge = pl.pallas_call(
        near_kernel,
        out_shape=(
            jax.ShapeDtypeStruct((3, 5, BS, BS), jnp.float32),
            jax.ShapeDtypeStruct((4, BS, BS), jnp.bfloat16),
        ),
        in_specs=[VMEM] * 5,
        out_specs=(VMEM, VMEM),
        scratch_shapes=[pltpu.VMEM((4, 2 * BS, 2 * BS), jnp.bfloat16)],
        compiler_params=params,
        cost_estimate=pl.CostEstimate(flops=2 * 10**10, bytes_accessed=10**8, transcendentals=0),
        name="near",
    )(lhs, left, side, packed, two)
    cross = []
    for i in range(0, count, 4):
        cross.append((i, (i - 4) % count))
        cross.append((i + 3, (i + 7) % count))
    got = lax.ppermute(edge, axes, cross)
    sums = pl.pallas_call(
        rest_kernel,
        out_shape=jax.ShapeDtypeStruct((4, 15, 32, BS), jnp.bfloat16),
        in_specs=[VMEM] * 6,
        out_specs=VMEM,
        scratch_shapes=[
            pltpu.VMEM((3, 5, BS, BS), jnp.float32),
            pltpu.VMEM((4, 2 * BS, 2 * BS), jnp.bfloat16),
        ],
        compiler_params=params,
        cost_estimate=pl.CostEstimate(flops=2 * 10**8, bytes_accessed=3 * 10**6, transcendentals=0),
        name="rest",
    )(lhs, left, near, side, packed, one)
    joined = pl.pallas_call(
        join_kernel,
        out_shape=jax.ShapeDtypeStruct((4, 15, 32, BS), jnp.bfloat16),
        in_specs=[VMEM, VMEM, VMEM],
        out_specs=VMEM,
        compiler_params=params,
        name="join",
    )(side, got, sums)
    parts = lax.all_to_all(joined, "grp", 0, 0, tiled=True)
    return pl.pallas_call(
        band_kernel,
        out_shape=jax.ShapeDtypeStruct((4, 7, 32, BS), jnp.float32),
        in_specs=[VMEM],
        out_specs=HBM,
        scratch_shapes=[
            pltpu.VMEM((4, 7, 32, BS), jnp.float32),
            pltpu.SemaphoreType.DMA((8,)),
        ],
        compiler_params=params,
        name="band",
    )(parts)


def solution(mesh):
    in_specs = (
        P(("rows", "grp"), None, None, None),
        P(("rows", "grp"), None),
        P(("rows", "grp"), None, None),
        P(("rows", "grp")),
    )
    out_specs = P("rows", None, "grp", None)
    return jax.shard_map(shards, mesh=mesh, in_specs=in_specs, out_specs=out_specs, check_vma=False)
```

```python
import functools

import jax
import jax.numpy as jnp
from jax import lax
from jax.experimental import pallas as pl
from jax.experimental.pallas import tpu as pltpu
from jax.sharding import PartitionSpec as P

BS = 128
RB = 4
KT = 12
HALO = RB * BS + 16
HBM = pl.BlockSpec(memory_space=pltpu.HBM)
VMEM = pl.BlockSpec(memory_space=pltpu.VMEM)
LIMIT = 32 << 20


def row_bits(count, agg_ref):
    first = agg_ref[0]
    low = (agg_ref[1] - first) & (count - 1)
    high = ((agg_ref[2] - first) & (count - 1)) - 1
    return low, high


def pack_kernel(count, agg_hbm, p_hbm, out_ref, agg_ref, agg_sem, p_sem):
    agg_copy = pltpu.make_async_copy(agg_hbm, agg_ref, agg_sem)
    agg_copy.start()
    copies = [
        pltpu.make_async_copy(p_hbm.at[r], out_ref.at[pl.ds(r * BS, BS)], p_sem.at[r])
        for r in range(RB)
    ]
    for copy in copies:
        copy.start()
    agg_copy.wait()
    low, high = row_bits(count, agg_ref)
    half = lax.broadcasted_iota(jnp.int32, (16, BS), 0) < 8
    out_ref[RB * BS :, :] = jnp.where(half, low, high).astype(jnp.float32).astype(jnp.bfloat16)
    for copy in copies:
        copy.wait()


def extend_kernel(
    count, cols_hbm, agg_hbm, a_hbm, p_ref, out_ref, lhs_ref, left, side_ref,
    cols_ref, agg_ref, place, tiles, sems, a_sems,
):
    cols_copy = pltpu.make_async_copy(cols_hbm, cols_ref, sems.at[0])
    agg_copy = pltpu.make_async_copy(agg_hbm, agg_ref, sems.at[1])
    cols_copy.start()
    agg_copy.start()
    copies = [
        pltpu.make_async_copy(a_hbm.at[r, pl.ds(3 * h, 3)], tiles.at[r, pl.ds(3 * h, 3)], a_sems.at[r, h])
        for r in range(RB)
        for h in range(4)
    ]
    for copy in copies:
        copy.start()
    out_ref[:HALO, :] = p_ref[...]
    agg_copy.wait()
    first = agg_ref[0]
    low, high = row_bits(count, agg_ref)
    turned = [p_ref[r * BS : (r + 1) * BS, :].astype(jnp.float32).T for r in range(RB)]
    zero = jnp.zeros((BS, BS), jnp.bfloat16)
    keep1 = (low == 0).astype(jnp.float32)
    keep2 = (high == 0).astype(jnp.float32)
    left[0, :BS, :BS] = turned[0].astype(jnp.bfloat16)
    left[0, :BS, BS:] = (turned[1] * keep1).astype(jnp.bfloat16)
    left[0, BS:, :BS] = zero
    left[0, BS:, BS:] = (turned[1] * (1 - keep1)).astype(jnp.bfloat16)
    left[1, :BS, :BS] = (turned[2] * keep2).astype(jnp.bfloat16)
    left[1, :BS, BS:] = zero
    left[1, BS:, :BS] = (turned[2] * (1 - keep2)).astype(jnp.bfloat16)
    left[1, BS:, BS:] = turned[3].astype(jnp.bfloat16)
    group_place = (first + 1) & 3
    side_ref[...] = jnp.full((8, BS), group_place, jnp.int32).astype(jnp.float32)
    cols_copy.wait()
    for r in range(RB):
        for k in range(KT):
            place[r, (cols_ref[r, k] - first * RB) & (RB * count - 1)] = k
    odd = (first + 1) & 1
    inner = (1 - odd) * 2 * RB
    outer = odd * 2 * RB
    for r in range(RB):
        for copy in copies[4 * r : 4 * r + 4]:
            copy.wait()
        for i in range(6):
            start = (RB, inner, outer)[i // 2] + 2 * (i % 2)
            for c in range(2):
                lhs_ref[i, r * BS : (r + 1) * BS, c * BS : (c + 1) * BS] = tiles[r, place[r, start + c]]
    h = group_place // 2
    border = jnp.where((group_place == 0) | (group_place == 3), 1, 0).astype(jnp.float32)
    part = left[h, pl.ds(pl.multiple_of(h * BS, BS), BS), :]
    rows = pl.ds(pl.multiple_of(h * 2 * BS, 2 * BS), 2 * BS)
    for i in range(2):
        both = jnp.dot(part, lhs_ref[4 + i, rows, :], preferred_element_type=jnp.float32) * border
        for c in range(2):
            to = HALO + (2 * i + c) * BS
            out_ref[to : to + BS, :] = both[:, c * BS : (c + 1) * BS].astype(jnp.bfloat16)


def halo_bits(ref):
    flags = ref[RB * BS : HALO, :].astype(jnp.float32)
    return (
        jnp.max(flags[:8, :]).astype(jnp.int32),
        jnp.max(flags[8:, :]).astype(jnp.int32),
    )


def fill_weights(w, tiles_ref, top):
    w[:BS, :BS] = tiles_ref[top * BS : (top + 1) * BS, :]
    w[BS:, BS:] = tiles_ref[(top + 1) * BS : (top + 2) * BS, :]


def clear_weights(weights):
    zero = jnp.zeros((BS, BS), jnp.bfloat16)
    for i in range(weights.shape[0]):
        weights[i, :BS, BS:] = zero
        weights[i, BS:, :BS] = zero


def add_pair(n, top, bits, lhs, w, left, acc):
    prod = jnp.dot(lhs, w[...], preferred_element_type=jnp.float32).astype(jnp.bfloat16)
    up = jnp.dot(left[0], prod[: 2 * BS], preferred_element_type=jnp.float32)
    down = jnp.dot(left[1], prod[2 * BS :], preferred_element_type=jnp.float32)
    slots = pair_slots(n, top, bits)
    for c in range(2):
        lanes = slice(c * BS, (c + 1) * BS)
        acc[0, slots[c]] += up[:BS, lanes]
        acc[1, slots[c]] += up[BS:, lanes] + down[:BS, lanes]
        acc[2, slots[c]] += down[BS:, lanes]


def pair_slots(n, top, bits):
    b1, b2 = bits
    return (n, n + b1) if top == 0 else (n + 1 + b2, n + 2)


def near_kernel(lhs_ref, left, side_ref, p_ref, two_ref, acc, edge_ref, weights):
    clear_weights(weights)
    for i in range(4):
        fill_weights(weights.at[i], (p_ref, two_ref)[i // 2], 2 * (i % 2))
    acc[...] = jnp.zeros_like(acc)
    side = jnp.max(side_ref[...]).astype(jnp.int32)
    own_bits, two_bits = halo_bits(p_ref), halo_bits(two_ref)
    for i in range(4):
        n = 1 if i < 2 else 2 - 2 * (side & 1)
        add_pair(n, 2 * (i % 2), own_bits if i < 2 else two_bits, lhs_ref[i], weights.at[i], left, acc)
    lower = side_ref[:1, :] < 2
    for j in range(4):
        edge_ref[j] = jnp.where(lower, acc[0, j + 1], acc[2, j]).astype(jnp.bfloat16)


def rest_kernel(lhs_ref, left, near, side_ref, p_ref, one_ref, out_ref, acc, weights):
    clear_weights(weights)
    for i in range(2):
        fill_weights(weights.at[i], one_ref, 2 * i)
        fill_weights(weights.at[2 + i], p_ref, 2 * i)
    acc[...] = near[...]
    side = jnp.max(side_ref[...]).astype(jnp.int32)
    bits = halo_bits(one_ref)
    own_bits = halo_bits(p_ref)
    for i in range(2):
        add_pair(2 * (side & 1), 2 * i, bits, lhs_ref[4 + i], weights.at[i], left, acc)
        both = jnp.concatenate(
            [one_ref[HALO + (2 * i + c) * BS : HALO + (2 * i + c + 1) * BS, :] for c in range(2)], axis=1
        )
        sums = jnp.dot(both, weights[2 + i], preferred_element_type=jnp.float32)
        slots = pair_slots(1, 2 * i, own_bits)
        for c in range(2):
            acc[1, slots[c]] += sums[:, c * BS : (c + 1) * BS]
    for s in range(3):
        for j in range(5):
            block = acc[s, j].astype(jnp.bfloat16)
            for q in range(4):
                out_ref[q, s * 5 + j] = block[q * 32 : (q + 1) * 32, :]


def join_kernel(side_ref, got_ref, sums_ref, out_ref):
    for side, base, shift in ((0, 0, 1), (3, 10, 0)):
        here = side_ref[:1, :] == side
        for j in range(5):
            for q in range(4):
                old = sums_ref[q, base + j].astype(jnp.float32)
                if 0 <= j - shift < 4:
                    new = got_ref[j - shift, q * 32 : (q + 1) * 32, :].astype(jnp.float32)
                else:
                    new = jnp.zeros_like(old)
                out_ref[q, base + j] = jnp.where(here, new, old).astype(jnp.bfloat16)
    for q in range(4):
        out_ref[q, 5:10] = sums_ref[q, 5:10]


def band_kernel(in_ref, out_hbm, out_ref, sems):
    def part(g, s, j):
        return in_ref[g, 5 * s + j].astype(jnp.float32)

    copies = []
    for c in range(4):
        for j in range(7):
            terms = []
            if 1 <= j < 6:
                terms.append(part(c, 1, j - 1))
            if j < 5:
                terms.append(part(c - 1, 2, j) if c > 0 else part(3, 2, j))
            if j >= 2:
                terms.append(part(c + 1, 0, j - 2) if c < 3 else part(0, 0, j - 2))
            total = terms[0]
            for term in terms[1:]:
                total = total + term
            out_ref[c, j] = total
            if j in (2, 6):
                here = pl.ds(0, 3) if j == 2 else pl.ds(3, 4)
                sem = sems.at[2 * c + j // 6]
                copies.append(pltpu.make_async_copy(out_ref.at[c, here], out_hbm.at[c, here], sem))
                copies[-1].start()
    for copy in copies:
        copy.wait()


def shards(a_tiles, a_cols, p_tiles, p_agg):
    axes = ("rows", "grp")
    count = lax.axis_size(axes)
    params = pltpu.CompilerParams(vmem_limit_bytes=LIMIT)
    a_tiles, a_cols, p_tiles, p_agg = (
        pltpu.with_memory_space_constraint(x, pltpu.HBM) for x in (a_tiles, a_cols, p_tiles, p_agg)
    )
    packed = pl.pallas_call(
        functools.partial(pack_kernel, count),
        out_shape=jax.ShapeDtypeStruct((HALO, BS), jnp.bfloat16),
        in_specs=[HBM, HBM],
        out_specs=VMEM,
        scratch_shapes=[
            pltpu.SMEM((RB,), jnp.int32),
            pltpu.SemaphoreType.DMA,
            pltpu.SemaphoreType.DMA((RB,)),
        ],
        compiler_params=params,
        name="pack",
    )(p_agg, p_tiles)
    two = lax.ppermute(packed, axes, [(i, i ^ 1) for i in range(count)])
    wide, lhs, left, side = pl.pallas_call(
        functools.partial(extend_kernel, count),
        out_shape=(
            jax.ShapeDtypeStruct((HALO + RB * BS, BS), jnp.bfloat16),
            jax.ShapeDtypeStruct((6, RB * BS, 2 * BS), jnp.bfloat16),
            jax.ShapeDtypeStruct((2, 2 * BS, 2 * BS), jnp.bfloat16),
            jax.ShapeDtypeStruct((8, BS), jnp.float32),
        ),
        in_specs=[HBM, HBM, HBM, VMEM],
        out_specs=(VMEM, VMEM, VMEM, VMEM),
        scratch_shapes=[
            pltpu.SMEM((RB, KT), jnp.int32),
            pltpu.SMEM((RB,), jnp.int32),
            pltpu.SMEM((RB, KT), jnp.int32),
            pltpu.VMEM((RB, KT, BS, BS), jnp.bfloat16),
            pltpu.SemaphoreType.DMA((2,)),
            pltpu.SemaphoreType.DMA((RB, 4)),
        ],
        compiler_params=params,
        name="extend",
    )(a_cols, p_agg, a_tiles, packed)
    one = lax.ppermute(wide, axes, [(i, (i + 1 if i % 2 else i - 1) % count) for i in range(count)])
    near, edge = pl.pallas_call(
        near_kernel,
        out_shape=(
            jax.ShapeDtypeStruct((3, 5, BS, BS), jnp.float32),
            jax.ShapeDtypeStruct((4, BS, BS), jnp.bfloat16),
        ),
        in_specs=[VMEM] * 5,
        out_specs=(VMEM, VMEM),
        scratch_shapes=[pltpu.VMEM((4, 2 * BS, 2 * BS), jnp.bfloat16)],
        compiler_params=params,
        cost_estimate=pl.CostEstimate(flops=2 * 10**10, bytes_accessed=10**8, transcendentals=0),
        name="near",
    )(lhs, left, side, packed, two)
    cross = []
    for i in range(0, count, 4):
        cross.append((i, (i - 4) % count))
        cross.append((i + 3, (i + 7) % count))
    got = lax.ppermute(edge, axes, cross)
    sums = pl.pallas_call(
        rest_kernel,
        out_shape=jax.ShapeDtypeStruct((4, 15, 32, BS), jnp.bfloat16),
        in_specs=[VMEM] * 6,
        out_specs=VMEM,
        scratch_shapes=[
            pltpu.VMEM((3, 5, BS, BS), jnp.float32),
            pltpu.VMEM((4, 2 * BS, 2 * BS), jnp.bfloat16),
        ],
        compiler_params=params,
        cost_estimate=pl.CostEstimate(flops=2 * 10**8, bytes_accessed=3 * 10**6, transcendentals=0),
        name="rest",
    )(lhs, left, near, side, packed, one)
    joined = pl.pallas_call(
        join_kernel,
        out_shape=jax.ShapeDtypeStruct((4, 15, 32, BS), jnp.bfloat16),
        in_specs=[VMEM, VMEM, VMEM],
        out_specs=VMEM,
        compiler_params=params,
        name="join",
    )(side, got, sums)
    parts = lax.all_to_all(joined, "grp", 0, 0, tiled=True)
    return pl.pallas_call(
        band_kernel,
        out_shape=jax.ShapeDtypeStruct((4, 7, 32, BS), jnp.float32),
        in_specs=[VMEM],
        out_specs=HBM,
        scratch_shapes=[
            pltpu.VMEM((4, 7, 32, BS), jnp.float32),
            pltpu.SemaphoreType.DMA((8,)),
        ],
        compiler_params=params,
        name="band",
    )(parts)


def solution(mesh):
    in_specs = (
        P(("rows", "grp"), None, None, None),
        P(("rows", "grp"), None),
        P(("rows", "grp"), None, None),
        P(("rows", "grp")),
    )
    out_specs = P("rows", None, "grp", None)
    return jax.shard_map(shards, mesh=mesh, in_specs=in_specs, out_specs=out_specs, check_vma=False)
```

```python
import functools

import jax
import jax.numpy as jnp
from jax import lax
from jax.experimental import pallas as pl
from jax.experimental.pallas import tpu as pltpu
from jax.sharding import PartitionSpec as P

BS = 128
RB = 4
KT = 12
HALO = RB * BS + 16
HBM = pl.BlockSpec(memory_space=pltpu.HBM)
VMEM = pl.BlockSpec(memory_space=pltpu.VMEM)
LIMIT = 32 << 20


def row_bits(count, agg_ref):
    first = agg_ref[0]
    low = (agg_ref[1] - first) & (count - 1)
    high = ((agg_ref[2] - first) & (count - 1)) - 1
    return low, high


def pack_kernel(count, agg_hbm, p_hbm, a_hbm, out_ref, tiles_ref, agg_ref, agg_sem, p_sem, a_sems):
    agg_copy = pltpu.make_async_copy(agg_hbm, agg_ref, agg_sem)
    agg_copy.start()
    copies = [
        pltpu.make_async_copy(p_hbm.at[r], out_ref.at[pl.ds(r * BS, BS)], p_sem.at[r])
        for r in range(RB)
    ]
    copies += [
        pltpu.make_async_copy(a_hbm.at[r, pl.ds(6 * h, 6)], tiles_ref.at[r, pl.ds(6 * h, 6)], a_sems.at[r, h])
        for r in range(2)
        for h in range(2)
    ]
    for copy in copies:
        copy.start()
    agg_copy.wait()
    low, high = row_bits(count, agg_ref)
    half = lax.broadcasted_iota(jnp.int32, (16, BS), 0) < 8
    out_ref[RB * BS :, :] = jnp.where(half, low, high).astype(jnp.float32).astype(jnp.bfloat16)
    for copy in copies:
        copy.wait()


def extend_kernel(
    count, cols_hbm, agg_hbm, a_hbm, p_ref, head_ref, out_ref, lhs_ref, left, side_ref,
    cols_ref, agg_ref, place, tiles, sems, a_sems,
):
    cols_copy = pltpu.make_async_copy(cols_hbm, cols_ref, sems.at[0])
    agg_copy = pltpu.make_async_copy(agg_hbm, agg_ref, sems.at[1])
    cols_copy.start()
    agg_copy.start()
    copies = [
        pltpu.make_async_copy(a_hbm.at[2 + r, pl.ds(6 * h, 6)], tiles.at[r, pl.ds(6 * h, 6)], a_sems.at[r, h])
        for r in range(2)
        for h in range(2)
    ]
    for copy in copies:
        copy.start()
    out_ref[:HALO, :] = p_ref[...]
    agg_copy.wait()
    first = agg_ref[0]
    low, high = row_bits(count, agg_ref)
    turned = [p_ref[r * BS : (r + 1) * BS, :].astype(jnp.float32).T for r in range(RB)]
    zero = jnp.zeros((BS, BS), jnp.bfloat16)
    keep1 = (low == 0).astype(jnp.float32)
    keep2 = (high == 0).astype(jnp.float32)
    left[0, :BS, :BS] = turned[0].astype(jnp.bfloat16)
    left[0, :BS, BS:] = (turned[1] * keep1).astype(jnp.bfloat16)
    left[0, BS:, :BS] = zero
    left[0, BS:, BS:] = (turned[1] * (1 - keep1)).astype(jnp.bfloat16)
    left[1, :BS, :BS] = (turned[2] * keep2).astype(jnp.bfloat16)
    left[1, :BS, BS:] = zero
    left[1, BS:, :BS] = (turned[2] * (1 - keep2)).astype(jnp.bfloat16)
    left[1, BS:, BS:] = turned[3].astype(jnp.bfloat16)
    group_place = (first + 1) & 3
    side_ref[...] = jnp.full((8, BS), group_place, jnp.int32).astype(jnp.float32)
    cols_copy.wait()
    for r in range(RB):
        for k in range(KT):
            place[r, (cols_ref[r, k] - first * RB) & (RB * count - 1)] = k
    odd = (first + 1) & 1
    inner = (1 - odd) * 2 * RB
    outer = odd * 2 * RB
    for r in range(RB):
        if r == 2:
            for copy in copies:
                copy.wait()
        for i in range(6):
            start = (RB, inner, outer)[i // 2] + 2 * (i % 2)
            for c in range(2):
                tile = (head_ref if r < 2 else tiles)[r % 2, place[r, start + c]]
                lhs_ref[i, r * BS : (r + 1) * BS, c * BS : (c + 1) * BS] = tile
    h = group_place // 2
    border = jnp.where((group_place == 0) | (group_place == 3), 1, 0).astype(jnp.float32)
    part = left[h, pl.ds(pl.multiple_of(h * BS, BS), BS), :]
    rows = pl.ds(pl.multiple_of(h * 2 * BS, 2 * BS), 2 * BS)
    for i in range(2):
        both = jnp.dot(part, lhs_ref[4 + i, rows, :], preferred_element_type=jnp.float32) * border
        for c in range(2):
            to = HALO + (2 * i + c) * BS
            out_ref[to : to + BS, :] = both[:, c * BS : (c + 1) * BS].astype(jnp.bfloat16)


def halo_bits(ref):
    flags = ref[RB * BS : HALO, :].astype(jnp.float32)
    return (
        jnp.max(flags[:8, :]).astype(jnp.int32),
        jnp.max(flags[8:, :]).astype(jnp.int32),
    )


def fill_weights(w, tiles_ref, top):
    w[:BS, :BS] = tiles_ref[top * BS : (top + 1) * BS, :]
    w[BS:, BS:] = tiles_ref[(top + 1) * BS : (top + 2) * BS, :]


def clear_weights(weights):
    zero = jnp.zeros((BS, BS), jnp.bfloat16)
    for i in range(weights.shape[0]):
        weights[i, :BS, BS:] = zero
        weights[i, BS:, :BS] = zero


def add_pair(n, top, bits, lhs, w, left, acc):
    prod = jnp.dot(lhs, w[...], preferred_element_type=jnp.float32).astype(jnp.bfloat16)
    up = jnp.dot(left[0], prod[: 2 * BS], preferred_element_type=jnp.float32)
    down = jnp.dot(left[1], prod[2 * BS :], preferred_element_type=jnp.float32)
    slots = pair_slots(n, top, bits)
    for c in range(2):
        lanes = slice(c * BS, (c + 1) * BS)
        acc[0, slots[c]] += up[:BS, lanes]
        acc[1, slots[c]] += up[BS:, lanes] + down[:BS, lanes]
        acc[2, slots[c]] += down[BS:, lanes]


def pair_slots(n, top, bits):
    b1, b2 = bits
    return (n, n + b1) if top == 0 else (n + 1 + b2, n + 2)


def near_kernel(lhs_ref, left, side_ref, p_ref, two_ref, acc, edge_ref, weights):
    clear_weights(weights)
    for i in range(4):
        fill_weights(weights.at[i], (p_ref, two_ref)[i // 2], 2 * (i % 2))
    acc[...] = jnp.zeros_like(acc)
    side = jnp.max(side_ref[...]).astype(jnp.int32)
    own_bits, two_bits = halo_bits(p_ref), halo_bits(two_ref)
    for i in range(4):
        n = 1 if i < 2 else 2 - 2 * (side & 1)
        add_pair(n, 2 * (i % 2), own_bits if i < 2 else two_bits, lhs_ref[i], weights.at[i], left, acc)
    lower = side_ref[:1, :] < 2
    for j in range(4):
        edge_ref[j] = jnp.where(lower, acc[0, j + 1], acc[2, j]).astype(jnp.bfloat16)


def rest_kernel(lhs_ref, left, near, side_ref, p_ref, one_ref, out_ref, acc, weights):
    clear_weights(weights)
    for i in range(2):
        fill_weights(weights.at[i], one_ref, 2 * i)
        fill_weights(weights.at[2 + i], p_ref, 2 * i)
    acc[...] = near[...]
    side = jnp.max(side_ref[...]).astype(jnp.int32)
    bits = halo_bits(one_ref)
    own_bits = halo_bits(p_ref)
    for i in range(2):
        add_pair(2 * (side & 1), 2 * i, bits, lhs_ref[4 + i], weights.at[i], left, acc)
        both = jnp.concatenate(
            [one_ref[HALO + (2 * i + c) * BS : HALO + (2 * i + c + 1) * BS, :] for c in range(2)], axis=1
        )
        sums = jnp.dot(both, weights[2 + i], preferred_element_type=jnp.float32)
        slots = pair_slots(1, 2 * i, own_bits)
        for c in range(2):
            acc[1, slots[c]] += sums[:, c * BS : (c + 1) * BS]
    for s in range(3):
        for j in range(5):
            block = acc[s, j].astype(jnp.bfloat16)
            for q in range(4):
                out_ref[q, s * 5 + j] = block[q * 32 : (q + 1) * 32, :]


def join_kernel(side_ref, got_ref, sums_ref, out_ref):
    for side, base, shift in ((0, 0, 1), (3, 10, 0)):
        here = side_ref[:1, :] == side
        for j in range(5):
            for q in range(4):
                old = sums_ref[q, base + j].astype(jnp.float32)
                if 0 <= j - shift < 4:
                    new = got_ref[j - shift, q * 32 : (q + 1) * 32, :].astype(jnp.float32)
                else:
                    new = jnp.zeros_like(old)
                out_ref[q, base + j] = jnp.where(here, new, old).astype(jnp.bfloat16)
    for q in range(4):
        out_ref[q, 5:10] = sums_ref[q, 5:10]


def band_kernel(in_ref, out_hbm, out_ref, sems):
    def part(g, s, j):
        return in_ref[g, 5 * s + j].astype(jnp.float32)

    copies = []
    for c in range(4):
        for j in range(7):
            terms = []
            if 1 <= j < 6:
                terms.append(part(c, 1, j - 1))
            if j < 5:
                terms.append(part(c - 1, 2, j) if c > 0 else part(3, 2, j))
            if j >= 2:
                terms.append(part(c + 1, 0, j - 2) if c < 3 else part(0, 0, j - 2))
            total = terms[0]
            for term in terms[1:]:
                total = total + term
            out_ref[c, j] = total
            if j in (2, 6):
                here = pl.ds(0, 3) if j == 2 else pl.ds(3, 4)
                sem = sems.at[2 * c + j // 6]
                copies.append(pltpu.make_async_copy(out_ref.at[c, here], out_hbm.at[c, here], sem))
                copies[-1].start()
    for copy in copies:
        copy.wait()


def shards(a_tiles, a_cols, p_tiles, p_agg):
    axes = ("rows", "grp")
    count = lax.axis_size(axes)
    params = pltpu.CompilerParams(vmem_limit_bytes=LIMIT)
    a_tiles, a_cols, p_tiles, p_agg = (
        pltpu.with_memory_space_constraint(x, pltpu.HBM) for x in (a_tiles, a_cols, p_tiles, p_agg)
    )
    packed, head = pl.pallas_call(
        functools.partial(pack_kernel, count),
        out_shape=(
            jax.ShapeDtypeStruct((HALO, BS), jnp.bfloat16),
            jax.ShapeDtypeStruct((2, KT, BS, BS), jnp.bfloat16),
        ),
        in_specs=[HBM, HBM, HBM],
        out_specs=(VMEM, VMEM),
        scratch_shapes=[
            pltpu.SMEM((RB,), jnp.int32),
            pltpu.SemaphoreType.DMA,
            pltpu.SemaphoreType.DMA((RB,)),
            pltpu.SemaphoreType.DMA((2, 2)),
        ],
        compiler_params=params,
        name="pack",
    )(p_agg, p_tiles, a_tiles)
    two = lax.ppermute(packed, axes, [(i, i ^ 1) for i in range(count)])
    wide, lhs, left, side = pl.pallas_call(
        functools.partial(extend_kernel, count),
        out_shape=(
            jax.ShapeDtypeStruct((HALO + RB * BS, BS), jnp.bfloat16),
            jax.ShapeDtypeStruct((6, RB * BS, 2 * BS), jnp.bfloat16),
            jax.ShapeDtypeStruct((2, 2 * BS, 2 * BS), jnp.bfloat16),
            jax.ShapeDtypeStruct((8, BS), jnp.float32),
        ),
        in_specs=[HBM, HBM, HBM, VMEM, VMEM],
        out_specs=(VMEM, VMEM, VMEM, VMEM),
        scratch_shapes=[
            pltpu.SMEM((RB, KT), jnp.int32),
            pltpu.SMEM((RB,), jnp.int32),
            pltpu.SMEM((RB, KT), jnp.int32),
            pltpu.VMEM((2, KT, BS, BS), jnp.bfloat16),
            pltpu.SemaphoreType.DMA((2,)),
            pltpu.SemaphoreType.DMA((2, 2)),
        ],
        compiler_params=params,
        name="extend",
    )(a_cols, p_agg, a_tiles, packed, head)
    one = lax.ppermute(wide, axes, [(i, (i + 1 if i % 2 else i - 1) % count) for i in range(count)])
    near, edge = pl.pallas_call(
        near_kernel,
        out_shape=(
            jax.ShapeDtypeStruct((3, 5, BS, BS), jnp.float32),
            jax.ShapeDtypeStruct((4, BS, BS), jnp.bfloat16),
        ),
        in_specs=[VMEM] * 5,
        out_specs=(VMEM, VMEM),
        scratch_shapes=[pltpu.VMEM((4, 2 * BS, 2 * BS), jnp.bfloat16)],
        compiler_params=params,
        cost_estimate=pl.CostEstimate(flops=2 * 10**10, bytes_accessed=10**8, transcendentals=0),
        name="near",
    )(lhs, left, side, packed, two)
    cross = []
    for i in range(0, count, 4):
        cross.append((i, (i - 4) % count))
        cross.append((i + 3, (i + 7) % count))
    got = lax.ppermute(edge, axes, cross)
    sums = pl.pallas_call(
        rest_kernel,
        out_shape=jax.ShapeDtypeStruct((4, 15, 32, BS), jnp.bfloat16),
        in_specs=[VMEM] * 6,
        out_specs=VMEM,
        scratch_shapes=[
            pltpu.VMEM((3, 5, BS, BS), jnp.float32),
            pltpu.VMEM((4, 2 * BS, 2 * BS), jnp.bfloat16),
        ],
        compiler_params=params,
        cost_estimate=pl.CostEstimate(flops=2 * 10**8, bytes_accessed=3 * 10**6, transcendentals=0),
        name="rest",
    )(lhs, left, near, side, packed, one)
    joined = pl.pallas_call(
        join_kernel,
        out_shape=jax.ShapeDtypeStruct((4, 15, 32, BS), jnp.bfloat16),
        in_specs=[VMEM, VMEM, VMEM],
        out_specs=VMEM,
        compiler_params=params,
        name="join",
    )(side, got, sums)
    parts = lax.all_to_all(joined, "grp", 0, 0, tiled=True)
    return pl.pallas_call(
        band_kernel,
        out_shape=jax.ShapeDtypeStruct((4, 7, 32, BS), jnp.float32),
        in_specs=[VMEM],
        out_specs=HBM,
        scratch_shapes=[
            pltpu.VMEM((4, 7, 32, BS), jnp.float32),
            pltpu.SemaphoreType.DMA((8,)),
        ],
        compiler_params=params,
        name="band",
    )(parts)


def solution(mesh):
    in_specs = (
        P(("rows", "grp"), None, None, None),
        P(("rows", "grp"), None),
        P(("rows", "grp"), None, None),
        P(("rows", "grp")),
    )
    out_specs = P("rows", None, "grp", None)
    return jax.shard_map(shards, mesh=mesh, in_specs=in_specs, out_specs=out_specs, check_vma=False)
```
